512 devices in a mesh: dp: 64 (over x, y, core), pool: 8 (over z).
Axes of the slice: x: 4, y: 8, z: 8, core: 2. Of those that a mesh axis runs over, the one named last changes fastest.
Arguments:
- query_act: bfloat16 [131072, 1024], P(('dp', 'pool')), may hold values from -6 to 6
- key_act: bfloat16 [131072, 1024], P(('dp', 'pool')), may hold values from -6 to 6
- value_act: bfloat16 [131072, 1024], P(('dp', 'pool')), may hold values from -6 to 6
- gate_act: bfloat16 [131072, 1024], P(('dp', 'pool')), may hold values from -6 to 6
- lengths: int32 [512, 4], P(('dp', 'pool')), may hold values from 1 to 192, 256 in all within a row
- targets: int32 [131072], P(('dp', 'pool')), may hold values from 0 to 767
- pool_rows: bfloat16 [49152, 1024], P(('dp', 'pool')), may hold values from -8 to 8
- pool_ids: int32 [49152], P(('dp', 'pool')), may hold values from 0 to 3071
- norm_gain: float32 [1024], replicated, may hold values from 0.1 to 1.9
Outputs:
- query_grad: bfloat16 [131072, 1024], P(('dp', 'pool'))
- key_grad: bfloat16 [131072, 1024], P(('dp', 'pool'))
- value_grad: bfloat16 [131072, 1024], P(('dp', 'pool'))
- gate_grad: bfloat16 [131072, 1024], P(('dp', 'pool'))
- pool_grad: float32 [49152, 1024], P(('dp', 'pool'))
- gain_grad: float32 [1024], replicated
The draws below stay inside these ranges and needn't reach their ends.
Inputs may be any that keep to these rules, and one draw needn't show every extreme that they name: In each device's row the 4 lengths sum to 256 and the longest is exactly 192.
All inputs are finite; a program needn't handle non-finite values.
Results may differ from the reference program's by a relative error of at most 0.015.
The reference program's roundings to bfloat16 on the way (of `attend`, `embedded`, `slopes`, `dmixed` and `dscores`) count: a program that leaves them out, or rounds other values in their place, can miss the bound.
Values may be sent and summed in bfloat16 or wider, within the bound.
No kernel may reach another device: no remote copies, remote signals or barrier semaphores. Data moves between devices by JAX's collectives and lax.ppermute only.
A program may use at most 64 MiB of HBM per device.

```python
import math
import jax
import jax.numpy as jnp
import numpy as np
from jax import lax

D = 1024
HEADS = 8
HEAD_DIM = 128
TOK_DEV = 256
SEQ_DEV = 4
LMAX = 192
NEG_POOL = 768
NEG_ALL = 49152
ITEMS = 3072
TOKENS = 131072
N_DP = 64
N_POOL = 8


def draw_pool_rows(key, part):
    key = jax.random.fold_in(key, 11)
    first, second = jax.random.split(key, 2)
    spread = jnp.exp(jax.random.uniform(second, (NEG_ALL, 1), jnp.float32, math.log(0.03), math.log(0.3)))
    result = jax.random.normal(first, (NEG_ALL, D), jnp.float32) * spread
    return jnp.clip(result, -8.0, 8.0).astype(jnp.bfloat16)


def set_ends(entries, stream_key, smallest, high):
    spot = [jax.random.randint(jax.random.fold_in(stream_key, axis), (), 0, length) for axis, length in enumerate(entries.shape)]
    widest = entries.shape.index(max(entries.shape))
    next_to = spot[:widest] + [(spot[widest] + 1) % entries.shape[widest]] + spot[widest + 1:]
    return entries.at[tuple(spot)].set(smallest).at[tuple(next_to)].set(high)


def block_levels(stream_key, extent, pieces, least, largest):
    def one(axis_at, blocks):
        heights = jax.random.uniform(jax.random.fold_in(jax.random.fold_in(stream_key, 6), axis_at), (blocks,), jnp.float32, least / len(pieces), largest / len(pieces))
        return jnp.repeat(jnp.exp(heights), extent[axis_at] // blocks).reshape((-1,) + (1,) * (len(extent) - axis_at - 1))

    loudness = one(*pieces[0])
    for cut in pieces[1:]:
        loudness = loudness * one(*cut)
    return loudness


def rank_table(amount, lean):
    loads = [(1 << 20) // math.isqrt(rank ** lean) + 1 for rank in range(1, amount + 1)]
    scale = 1 + sum(loads) // (1 << 30)
    return np.cumsum(np.array([max(1, weight // scale) for weight in loads]))


def ranked_ids(own_key, extent, count, skew):
    grid = rank_table(count, skew)
    ticket = jax.random.randint(jax.random.fold_in(own_key, 1), extent, 0, int(grid[count - 1]))
    rank = jnp.searchsorted(jnp.asarray(grid, jnp.int32), ticket, side="right")
    return jax.random.permutation(jax.random.fold_in(own_key, 2), count)[rank].astype(jnp.int32)


def length_profile(count, total, reach, skew):
    portions = [(1 << 20) // math.isqrt(grade ** skew) + 1 for grade in range(2, count + 1)]
    spare, counts = total - reach - (count - 1), [1] * (count - 1)
    while spare > 0:
        free = [i for i in range(count - 1) if counts[i] < reach]
        whole, budget = sum([portions[i] for i in free]), spare
        for i in free:
            addition = min(reach - counts[i], max(1, budget * portions[i] // whole), spare)
            counts[i] = counts[i] + addition
            spare = spare - addition
    return np.array([reach] + counts)


def uneven(key, number_of, total, most, lean):
    if number_of == 2:
        one = jax.random.randint(key, (), max(1, total - most), min(most, total - 1) + 1)
        return jnp.stack([one, total - one])
    tallies = jnp.asarray(length_profile(number_of, total, most, lean), jnp.int32)
    twos = (number_of - 1) // 2
    source_of, taker = tallies[1:1 + 2 * twos:2], tallies[2:2 + 2 * twos:2]
    margin = jnp.minimum(source_of - 1, most - taker)
    moved = jax.random.randint(jax.random.fold_in(key, 1), (twos,), 0, 1 << 20) % (margin + 1)
    tallies = tallies.at[1:1 + 2 * twos:2].set(source_of - moved).at[2:2 + 2 * twos:2].set(taker + moved)
    return tallies[jax.random.permutation(jax.random.fold_in(key, 2), number_of)]


def gaussian(own_key, dims, scale, most, shards=(), kind=jnp.bfloat16):
    drawn = jax.random.normal(own_key, dims, jnp.float32) * scale
    if len(shards) > 0:
        drawn = block_levels(own_key, dims, shards, -0.22, 0.18) * drawn
    return jnp.clip(drawn, min=-most, max=most).astype(kind)


def setup_inputs(seed: int = 0) -> dict:
    arg_keys = jax.random.split(jax.random.key(seed), 10)
    query_act = gaussian(arg_keys[0], (TOKENS, D), 1.0, 6.0, ((0, 512),))
    key_act = gaussian(arg_keys[1], (TOKENS, D), 1.0, 6.0, ((0, 512),))
    value_act = gaussian(arg_keys[2], (TOKENS, D), 1.0, 6.0, ((0, 512),))
    gate_act = gaussian(arg_keys[3], (TOKENS, D), 1.0, 6.0, ((0, 512),))
    lengths = jax.vmap(lambda own: uneven(own, SEQ_DEV, TOK_DEV, LMAX, 2))(jax.random.split(arg_keys[4], (N_DP * N_POOL))).reshape((N_DP * N_POOL, SEQ_DEV)).astype(jnp.int32)
    targets = set_ends(jax.random.randint(arg_keys[5], (TOKENS,), 0, NEG_POOL), jax.random.fold_in(arg_keys[5], 1), 0, NEG_POOL - 1).astype(jnp.int32)
    pool_rows = draw_pool_rows(jax.random.fold_in(arg_keys[9], 71), 0)
    pool_ids = set_ends(ranked_ids(arg_keys[7], (NEG_ALL,), ITEMS, 2), jax.random.fold_in(arg_keys[7], 3), 0, ITEMS - 1).astype(jnp.int32)
    norm_gain = jnp.clip(1.0 + 0.18 * jax.random.normal(arg_keys[8], (D,), jnp.float32), 0.1, 1.9)
    return dict(query_act=query_act, key_act=key_act, value_act=value_act, gate_act=gate_act, lengths=lengths, targets=targets, pool_rows=pool_rows, pool_ids=pool_ids, norm_gain=norm_gain)


EPSILON = 1e-05

def device_grads(query_act, key_act, value_act, gate_act, length_row, target_row, rows, row_ids, norm_gain):
    count = TOK_DEV
    scaling = HEAD_DIM ** (-0.5)
    finish = jnp.cumsum(length_row).astype(jnp.int32)
    position = jnp.arange(count, dtype=jnp.int32)
    segment = lax.optimization_barrier(jnp.sum((position[:, None] >= finish[None, :]).astype(jnp.int32), axis=1))
    following = lax.optimization_barrier(jnp.sum((position[:, None] + 1 >= finish[None, :]).astype(jnp.int32), axis=1))
    usable = (following == segment).astype(jnp.float32)
    allowed = (segment[:, None] == segment[None, :]) & (position[None, :] <= position[:, None])
    queries = query_act.astype(jnp.float32).reshape(count, HEADS, HEAD_DIM)
    keys_all = key_act.astype(jnp.float32).reshape(count, HEADS, HEAD_DIM)
    values_all = value_act.astype(jnp.float32).reshape(count, HEADS, HEAD_DIM)
    scores = jnp.einsum('thd,shd->hts', queries, keys_all) * scaling
    squash = jax.nn.sigmoid(scores)
    attend = jnp.where(allowed[None], scores * squash, 0.0) / LMAX
    attend_b = attend.astype(jnp.bfloat16)
    mixed = jnp.einsum('hts,shd->thd', attend_b.astype(jnp.float32), values_all).reshape(count, D)
    center = mixed - lax.optimization_barrier(jnp.mean(mixed, axis=1, keepdims=True))
    inv_dev = lax.rsqrt(lax.optimization_barrier(jnp.mean(center * center, axis=1, keepdims=True)) + EPSILON)
    normed = center * inv_dev
    scaled = normed * norm_gain
    gate_f = gate_act.astype(jnp.float32)
    embedded = (scaled * gate_f).astype(jnp.bfloat16)
    logits = jnp.dot(embedded, rows.T, preferred_element_type=jnp.float32)
    columns = jnp.arange(NEG_POOL, dtype=jnp.int32)
    chosen = target_row[:, None] == columns[None, :]
    target_ids = lax.optimization_barrier(jnp.sum(jnp.where(chosen, row_ids[None, :], 0), axis=1)).astype(jnp.int32)
    clash = (row_ids[None, :] == target_ids[:, None]) & jnp.logical_not(chosen)
    masked = jnp.where(clash, -1e+30, logits)
    peak = lax.optimization_barrier(jnp.max(masked, axis=1, keepdims=True))
    total = lax.optimization_barrier(jnp.sum(jnp.exp(masked - peak), axis=1, keepdims=True))
    log_total = peak + jnp.log(total)
    probs = jnp.where(clash, 0.0, jnp.exp(logits - log_total))
    slopes = (usable[:, None] * (probs - chosen.astype(jnp.float32))).astype(jnp.bfloat16)
    term = jnp.dot(slopes.T, embedded, preferred_element_type=jnp.float32)
    back = jnp.dot(slopes, rows, preferred_element_type=jnp.float32)
    dscaled = back * gate_f
    gate_grad = (back * scaled).astype(jnp.bfloat16)
    gain_part = lax.optimization_barrier(jnp.sum(dscaled * normed, axis=0))
    dnormed = dscaled * norm_gain
    dmixed = (dnormed - lax.optimization_barrier(jnp.mean(dnormed, axis=1, keepdims=True)) - normed * lax.optimization_barrier(jnp.mean(dnormed * normed, axis=1, keepdims=True))) * inv_dev
    dmixed_h = dmixed.astype(jnp.bfloat16).astype(jnp.float32).reshape(count, HEADS, HEAD_DIM)
    dattend = jnp.einsum('thd,shd->hts', dmixed_h, values_all)
    value_grad = jnp.einsum('hts,thd->shd', attend_b.astype(jnp.float32), dmixed_h).reshape(count, D).astype(jnp.bfloat16)
    dscores = jnp.where(allowed[None], dattend * squash * (1.0 + scores * (1.0 - squash)), 0.0) * (scaling / LMAX)
    dscores_f = dscores.astype(jnp.bfloat16).astype(jnp.float32)
    query_grad = jnp.einsum('hts,shd->thd', dscores_f, keys_all).reshape(count, D).astype(jnp.bfloat16)
    key_grad = jnp.einsum('hts,thd->shd', dscores_f, queries).reshape(count, D).astype(jnp.bfloat16)
    return (query_grad, key_grad, value_grad, gate_grad, gain_part, term)

def reference(query_act, key_act, value_act, gate_act, lengths, targets, pool_rows, pool_ids, norm_gain):
    shape4 = (N_DP, N_POOL, TOK_DEV, D)
    grouped = (query_act.reshape(shape4), key_act.reshape(shape4), value_act.reshape(shape4), gate_act.reshape(shape4), lengths.reshape(N_DP, N_POOL, SEQ_DEV), targets.reshape(N_DP, N_POOL, TOK_DEV), pool_rows.reshape(N_DP, NEG_POOL, D), pool_ids.reshape(N_DP, NEG_POOL))

    def one_group(item):
        rows = item[6]
        row_ids = item[7]

        def member(inner):
            return device_grads(inner[0], inner[1], inner[2], inner[3], inner[4], inner[5], rows, row_ids, norm_gain)
        outs = lax.map(member, item[:6])
        return (outs[0], outs[1], outs[2], outs[3], lax.optimization_barrier(jnp.sum(outs[4], axis=0)), lax.optimization_barrier(jnp.sum(outs[5], axis=0)))
    result = lax.map(one_group, grouped)
    query_grad = result[0].reshape(TOKENS, D)
    key_grad = result[1].reshape(TOKENS, D)
    value_grad = result[2].reshape(TOKENS, D)
    gate_grad = result[3].reshape(TOKENS, D)
    gain_grad = lax.optimization_barrier(jnp.sum(result[4], axis=0))
    pool_grad = result[5].reshape(NEG_ALL, D)
    return (query_grad, key_grad, value_grad, gate_grad, pool_grad, gain_grad)
```

```python
import functools

import jax
import jax.numpy as jnp
from jax import lax
from jax.experimental import pallas as pl
from jax.experimental.pallas import tpu as pltpu
from jax.sharding import PartitionSpec as P

HEADS = 8
LMAX = 192
EPSILON = 1e-05
COUNT = 256
WIDTH = 1024
HEAD_DIM = 128
ROWS = 96
RING = 8
POOL = ROWS * RING
HALF = ROWS // 2
XY = 32
NEAR = 16

F32 = jnp.float32
BF16 = jnp.bfloat16
I32 = jnp.int32
CONTRACT_LAST = (((1,), (1,)), ((), ()))
CONTRACT_FIRST = (((0,), (0,)), ((), ()))


def dot(a, b, dims=(((1,), (0,)), ((), ()))):
    return lax.dot_general(a, b, dims, preferred_element_type=F32)


def forward_kernel(
    lengths, q_ref, k_ref, v_ref, gate_ref, gain_ref,
    emb_ref, normed_ref, inv_ref, attend_ref, slope_ref, mixed, mask,
):
    scaling = HEAD_DIM ** (-0.5)
    row = lax.broadcasted_iota(I32, (COUNT, COUNT), 0)
    col = lax.broadcasted_iota(I32, (COUNT, COUNT), 1)
    first = jnp.zeros((COUNT, COUNT), I32)
    finish = jnp.int32(0)
    for i in range(lengths.shape[1]):
        finish = finish + lengths[0, i]
        first = jnp.where(row >= finish, finish, first)
    mask[...] = jnp.where((col >= first) & (col <= row), F32(1.0 / LMAX), F32(0.0))
    for h in range(HEADS):
        lanes = slice(h * HEAD_DIM, (h + 1) * HEAD_DIM)
        scores = dot(q_ref[:, lanes], k_ref[:, lanes], CONTRACT_LAST) * scaling
        squash = 0.5 * jnp.tanh(0.5 * scores) + 0.5
        keep = mask[...]
        act = scores * squash
        attend = (act * keep).astype(BF16)
        attend_ref[h] = attend
        slope_ref[h] = (squash + act * (1.0 - squash)) * (keep * scaling)
        mixed[:, lanes] = dot(attend, v_ref[:, lanes])
    gain = gain_ref[...]
    step = 64
    for i in range(COUNT // step):
        at = slice(i * step, (i + 1) * step)
        part = mixed[at, :]
        center = part - jnp.mean(part, axis=1, keepdims=True)
        inv = lax.rsqrt(jnp.mean(center * center, axis=1, keepdims=True) + EPSILON)
        normed = center * inv
        normed_ref[at, :] = normed
        inv_ref[at, :] = jnp.broadcast_to(inv, (step, HEAD_DIM))
        emb_ref[at, :] = (normed * gain * gate_ref[at, :].astype(F32)).astype(BF16)


def pool_kernel(
    place, lengths, emb_ref, normed_ref, inv_ref, gate_ref, gain_ref, target_ref, ids_ref,
    own, r1, r2, r3, l1, l2, l3, far_a, far_b,
    plus1, minus1, plus2h, minus2h, plus2, minus2, keep_ref, gate_grad_ref, dmixed_ref, part_ref,
    rows, logits, slopes, terms, back,
):
    z = place[0]

    def block(offset):
        return pl.multiple_of(lax.rem(z + offset + RING, RING) * ROWS, 16)

    rows[pl.ds(block(0), ROWS), :] = own[...]
    for offset, ref in ((-1, r1), (-2, r2), (-3, r3), (1, l1), (2, l2), (3, l3)):
        rows[pl.ds(block(offset), ROWS), :] = ref[...]
    rows[pl.ds(block(4), HALF), :] = far_a[...]
    rows[pl.ds(pl.multiple_of(block(4) + HALF, 16), HALF), :] = far_b[...]

    logits[...] = dot(emb_ref[...], rows[...], CONTRACT_LAST)
    step = 32
    ids = ids_ref[...]
    for i in range(COUNT // step):
        at = slice(i * step, (i + 1) * step)
        target = target_ref[at, :]
        column = lax.broadcasted_iota(I32, (step, POOL), 1)
        chosen = column == target
        own_id = jnp.sum(jnp.where(chosen, ids, F32(0)), axis=1, keepdims=True)
        token = lax.broadcasted_iota(I32, (step, 1), 0) + i * step
        usable = jnp.ones((step, 1), F32)
        finish = jnp.int32(0)
        for j in range(lengths.shape[1]):
            finish = finish + lengths[0, j]
            usable = jnp.where(token + 1 == finish, F32(0.0), usable)
        clash = (ids == own_id) & jnp.logical_not(chosen)
        masked = jnp.where(clash, F32(-1e30), logits[at, :])
        peak = jnp.max(masked, axis=1, keepdims=True)
        weight = jnp.where(clash, F32(0.0), jnp.exp(masked - peak))
        total = jnp.sum(weight, axis=1, keepdims=True)
        probs = weight * (1.0 / total)
        slopes[at, :] = (usable * jnp.where(chosen, probs - 1.0, probs)).astype(BF16)

    terms[...] = dot(slopes[...], emb_ref[...], CONTRACT_FIRST).astype(BF16)
    keep_ref[...] = terms[pl.ds(block(0), ROWS), :]
    plus1[0:ROWS, :] = terms[pl.ds(block(3), ROWS), :]
    plus1[ROWS : 2 * ROWS, :] = terms[pl.ds(block(1), ROWS), :]
    minus1[0:ROWS, :] = terms[pl.ds(block(-3), ROWS), :]
    minus1[ROWS : 2 * ROWS, :] = terms[pl.ds(block(-1), ROWS), :]
    plus2h[...] = terms[pl.ds(block(4), HALF), :]
    minus2h[...] = terms[pl.ds(pl.multiple_of(block(4) + HALF, 16), HALF), :]
    plus2[...] = terms[pl.ds(block(2), ROWS), :]
    minus2[...] = terms[pl.ds(block(-2), ROWS), :]

    back[...] = dot(slopes[...], rows[...])
    gain = gain_ref[...]
    sums = jnp.zeros((8, WIDTH), F32)
    step = 32
    for i in range(COUNT // step):
        at = slice(i * step, (i + 1) * step)
        normed = normed_ref[at, :]
        pulled = back[at, :]
        gate_grad_ref[at, :] = (pulled * (normed * gain)).astype(BF16)
        dscaled = pulled * gate_ref[at, :].astype(F32)
        product = dscaled * normed
        sums = sums + jnp.sum(product.reshape(step // 8, 8, WIDTH), axis=0)
        dnormed = dscaled * gain
        mean1 = jnp.mean(dnormed, axis=1, keepdims=True)
        mean2 = jnp.mean(product * gain, axis=1, keepdims=True)
        dmixed_ref[at, :] = ((dnormed - mean1 - normed * mean2) * inv_ref[at, 0:1]).astype(BF16)
    part_ref[...] = jnp.broadcast_to(jnp.sum(sums, axis=0, keepdims=True), (XY, WIDTH))


def backward_kernel(
    dmixed_ref, q_ref, k_ref, v_ref, attend_ref, slope_ref, dq_ref, dk_ref, dv_ref,
):
    for h in range(HEADS):
        lanes = slice(h * HEAD_DIM, (h + 1) * HEAD_DIM)
        dmixed = dmixed_ref[:, lanes]
        dattend = dot(dmixed, v_ref[:, lanes], CONTRACT_LAST)
        dscores = (dattend * slope_ref[h]).astype(BF16)
        dv_ref[:, lanes] = dot(attend_ref[h], dmixed, CONTRACT_FIRST).astype(BF16)
        dq_ref[:, lanes] = dot(dscores, k_ref[:, lanes]).astype(BF16)
        dk_ref[:, lanes] = dot(dscores, q_ref[:, lanes], CONTRACT_FIRST).astype(BF16)


VMEM = pl.BlockSpec(memory_space=pltpu.VMEM)
SMEM = pl.BlockSpec(memory_space=pltpu.SMEM)


def call(kernel, specs, outs, scratch, cost, limit=24):
    return pl.pallas_call(
        kernel,
        out_shape=[jax.ShapeDtypeStruct(shape, kind) for shape, kind in outs],
        in_specs=specs,
        out_specs=[VMEM] * len(outs),
        scratch_shapes=[pltpu.VMEM(shape, kind) for shape, kind in scratch],
        compiler_params=pltpu.CompilerParams(vmem_limit_bytes=limit * 1024 * 1024),
        cost_estimate=cost,
    )


def shift(value, by):
    return lax.ppermute(value, "pool", [(i, (i + by) % RING) for i in range(RING)])


def body(query_act, key_act, value_act, gate_act, lengths, targets, pool_rows, pool_ids, norm_gain):
    token = (COUNT, WIDTH)
    r2 = shift(pool_rows, 2)
    l2 = shift(pool_rows, -2)
    r1 = shift(pool_rows, 1)
    l1 = shift(pool_rows, -1)
    r3 = shift(r2, 1)
    l3 = shift(l2, -1)
    far_a = shift(r2[:HALF], 2)
    far_b = shift(l2[HALF:], -2)
    ids = lax.all_to_all(
        jnp.broadcast_to(pool_ids[None, :], (RING, ROWS)), "pool", 0, 0
    ).reshape(1, POOL).astype(F32)
    gain = norm_gain.reshape(1, WIDTH)
    place = lax.axis_index("pool").reshape(1).astype(I32)

    emb, normed, inv, attend, slope = call(
        forward_kernel,
        [SMEM] + [VMEM] * 5,
        [(token, BF16), (token, F32), ((COUNT, HEAD_DIM), F32),
         ((HEADS, COUNT, COUNT), BF16), ((HEADS, COUNT, COUNT), F32)],
        [(token, F32), ((COUNT, COUNT), F32)],
        pl.CostEstimate(flops=2 * 10**9, bytes_accessed=8 * 10**6, transcendentals=524288),
    )(lengths, query_act, key_act, value_act, gate_act, gain)

    chunk = (ROWS, WIDTH)
    half = (HALF, WIDTH)
    plus1, minus1, plus2h, minus2h, plus2, minus2, kept, gate_grad, dmixed, part = call(
        pool_kernel,
        [SMEM, SMEM] + [VMEM] * 16,
        [((2 * ROWS, WIDTH), BF16), ((2 * ROWS, WIDTH), BF16), (half, BF16), (half, BF16),
         (chunk, BF16), (chunk, BF16), (chunk, BF16), (token, BF16), (token, BF16),
         ((XY, WIDTH), F32)],
        [((POOL, WIDTH), BF16), ((COUNT, POOL), F32), ((COUNT, POOL), BF16),
         ((POOL, WIDTH), BF16), (token, F32)],
        pl.CostEstimate(flops=2 * 10**9, bytes_accessed=8 * 10**6, transcendentals=196608),
    )(place, lengths, emb, normed, inv, gate_act, gain, targets.reshape(COUNT, 1), ids,
      pool_rows, r1, r2, r3, l1, l2, l3, far_a, far_b)

    from_left = shift(plus1, 1)
    from_right = shift(minus1, -1)
    far_left = shift(plus2h, 2)
    far_right = shift(minus2h, -2)

    plane = [[x * 16 + y * 2 + c for x in range(4) for y in range(8)] for c in range(2)]
    spread = lax.all_to_all(part, "dp", 0, 0, axis_index_groups=plane)
    spread = jnp.broadcast_to(jnp.sum(spread, axis=0, keepdims=True), (NEAR, WIDTH))
    near = [[i * NEAR + j for j in range(NEAR)] for i in range(XY)]
    spread = lax.all_to_all(spread, ("dp", "pool"), 0, 0, axis_index_groups=near)
    gain_grad = jnp.sum(spread, axis=0)

    zeros = jnp.zeros(half, F32)
    plus2 = (
        plus2.astype(F32) + from_left[:ROWS].astype(F32)
        + jnp.concatenate([far_left.astype(F32), zeros])
    ).astype(BF16)
    minus2 = (
        minus2.astype(F32) + from_right[:ROWS].astype(F32)
        + jnp.concatenate([zeros, far_right.astype(F32)])
    ).astype(BF16)
    two_left = shift(plus2, 2)
    two_right = shift(minus2, -2)
    pool_grad = (
        kept.astype(F32) + from_left[ROWS:].astype(F32) + from_right[ROWS:].astype(F32)
        + two_left.astype(F32) + two_right.astype(F32)
    )

    query_grad, key_grad, value_grad = call(
        backward_kernel,
        [VMEM] * 6,
        [(token, BF16)] * 3,
        [],
        pl.CostEstimate(flops=2 * 10**9, bytes_accessed=8 * 10**6, transcendentals=0),
    )(dmixed, query_act, key_act, value_act, attend, slope)
    return (query_grad, key_grad, value_grad, gate_grad, pool_grad, gain_grad)


def solution(mesh):
    rows = P(("dp", "pool"), None)
    flat = P(("dp", "pool"))
    in_specs = (rows, rows, rows, rows, rows, flat, rows, flat, P())
    out_specs = (rows, rows, rows, rows, rows, P())
    return jax.shard_map(body, mesh=mesh, in_specs=in_specs, out_specs=out_specs, check_vma=False)
```

```python
import jax
import jax.numpy as jnp
from jax import lax
from jax.experimental import pallas as pl
from jax.experimental.pallas import tpu as pltpu
from jax.sharding import PartitionSpec as P

HEADS = 8
LMAX = 192
EPSILON = 1e-05
COUNT = 256
WIDTH = 1024
HEAD_DIM = 128
ROWS = 96
RING = 8
POOL = ROWS * RING
LIMIT = 56 * 1024 * 1024
XY = 32
NEAR = 16

F32 = jnp.float32
BF16 = jnp.bfloat16
I32 = jnp.int32
CONTRACT_LAST = (((1,), (1,)), ((), ()))
CONTRACT_FIRST = (((0,), (0,)), ((), ()))


def dot(a, b, dims=(((1,), (0,)), ((), ()))):
    return lax.dot_general(a, b, dims, preferred_element_type=F32)


def step_kernel(
    place, lengths, q_hbm, k_hbm, v_hbm, gate_hbm, gain_ref, target_ref, ids_ref,
    own, r1, r2, r3, l1, l2, l3, four,
    dq_hbm, dk_hbm, dv_hbm, gate_grad_hbm, part_ref,
    plus1, minus1, plus4, plus2, minus2, kept,
    q, k, v, gate, rows, attend, slope, mask, normed, inv, emb, logits, slopes, terms, back,
    dmixed, gate_grad, dq, dk, dv, came, went,
):
    z = place[0]

    def start_of(offset):
        return pl.multiple_of(lax.rem(z + offset + RING, RING) * ROWS, 16)

    def load(src, dst, i):
        copy = pltpu.make_async_copy(src, dst, came.at[i])
        copy.start()
        return copy

    stores = []

    def store(src, dst):
        copy = pltpu.make_async_copy(src, dst, went.at[len(stores)])
        copy.start()
        stores.append(copy)

    inputs = [load(*pair, i) for i, pair in enumerate(((q_hbm, q), (k_hbm, k), (v_hbm, v), (gate_hbm, gate)))]
    blocks = [
        load(ref, rows.at[pl.ds(start_of(offset), ROWS), :], 4 + i)
        for i, (offset, ref) in enumerate(
            ((0, own), (-1, r1), (-2, r2), (-3, r3), (1, l1), (2, l2), (3, l3), (4, four))
        )
    ]

    scaling = HEAD_DIM ** (-0.5)
    row = lax.broadcasted_iota(I32, (COUNT, COUNT), 0)
    col = lax.broadcasted_iota(I32, (COUNT, COUNT), 1)
    first = jnp.zeros((COUNT, COUNT), I32)
    finish = jnp.int32(0)
    for i in range(lengths.shape[1]):
        finish = finish + lengths[0, i]
        first = jnp.where(row >= finish, finish, first)
    mask[...] = jnp.where((col >= first) & (col <= row), F32(1.0 / LMAX), F32(0.0))
    for copy in inputs[:3]:
        copy.wait()
    for h in range(HEADS):
        lanes = slice(h * HEAD_DIM, (h + 1) * HEAD_DIM)
        scores = dot(q[:, lanes], k[:, lanes], CONTRACT_LAST) * scaling
        squash = 0.5 * jnp.tanh(0.5 * scores) + 0.5
        keep = mask[...]
        act = scores * squash
        weights = (act * keep).astype(BF16)
        attend[h] = weights
        slope[h] = (squash + act * (1.0 - squash)) * (keep * scaling)
        normed[:, lanes] = dot(weights, v[:, lanes])
    inputs[3].wait()
    gain = gain_ref[...]
    step = 32
    for i in range(COUNT // step):
        at = slice(i * step, (i + 1) * step)
        part = normed[at, :]
        center = part - jnp.mean(part, axis=1, keepdims=True)
        scale = lax.rsqrt(jnp.mean(center * center, axis=1, keepdims=True) + EPSILON)
        unit = center * scale
        normed[at, :] = unit
        inv[at, :] = jnp.broadcast_to(scale, (step, HEAD_DIM))
        emb[at, :] = (unit * gain * gate[at, :].astype(F32)).astype(BF16)

    for copy in blocks:
        copy.wait()
    logits[...] = dot(emb[...], rows[...], CONTRACT_LAST)
    ids = ids_ref[...]
    for i in range(COUNT // step):
        at = slice(i * step, (i + 1) * step)
        target = target_ref[at, :]
        column = lax.broadcasted_iota(I32, (step, POOL), 1)
        chosen = column == target
        own_id = jnp.sum(jnp.where(chosen, ids, F32(0)), axis=1, keepdims=True)
        token = lax.broadcasted_iota(I32, (step, 1), 0) + i * step
        usable = jnp.ones((step, 1), F32)
        finish = jnp.int32(0)
        for j in range(lengths.shape[1]):
            finish = finish + lengths[0, j]
            usable = jnp.where(token + 1 == finish, F32(0.0), usable)
        clash = (ids == own_id) & jnp.logical_not(chosen)
        masked = jnp.where(clash, F32(-1e30), logits[at, :])
        peak = jnp.max(masked, axis=1, keepdims=True)
        weight = jnp.where(clash, F32(0.0), jnp.exp(masked - peak))
        total = jnp.sum(weight, axis=1, keepdims=True)
        probs = weight * (1.0 / total)
        slopes[at, :] = (usable * jnp.where(chosen, probs - 1.0, probs)).astype(BF16)

    terms[...] = dot(slopes[...], emb[...], CONTRACT_FIRST).astype(BF16)
    for offset, ref in (
        (3, plus1.at[0:ROWS]), (1, plus1.at[ROWS : 2 * ROWS]),
        (-3, minus1.at[0:ROWS]), (-1, minus1.at[ROWS : 2 * ROWS]),
        (4, plus4), (2, plus2), (-2, minus2), (0, kept),
    ):
        store(terms.at[pl.ds(start_of(offset), ROWS), :], ref)

    back[...] = dot(slopes[...], rows[...])
    sums = jnp.zeros((8, WIDTH), F32)
    for i in range(COUNT // step):
        at = slice(i * step, (i + 1) * step)
        unit = normed[at, :]
        pulled = back[at, :]
        gate_grad[at, :] = (pulled * (unit * gain)).astype(BF16)
        dscaled = pulled * gate[at, :].astype(F32)
        product = dscaled * unit
        sums = sums + jnp.sum(product.reshape(step // 8, 8, WIDTH), axis=0)
        dnormed = dscaled * gain
        mean1 = jnp.mean(dnormed, axis=1, keepdims=True)
        mean2 = jnp.mean(product * gain, axis=1, keepdims=True)
        dmixed[at, :] = ((dnormed - mean1 - unit * mean2) * inv[at, 0:1]).astype(BF16)
    store(gate_grad, gate_grad_hbm)
    part = jnp.sum(sums, axis=0, keepdims=True)
    for i in range(XY):
        part_ref[i] = part

    for h in range(HEADS):
        lanes = slice(h * HEAD_DIM, (h + 1) * HEAD_DIM)
        part = dmixed[:, lanes]
        dattend = dot(part, v[:, lanes], CONTRACT_LAST)
        dscores = (dattend * slope[h]).astype(BF16)
        dv[:, lanes] = dot(attend[h], part, CONTRACT_FIRST).astype(BF16)
        dq[:, lanes] = dot(dscores, k[:, lanes]).astype(BF16)
        dk[:, lanes] = dot(dscores, q[:, lanes], CONTRACT_FIRST).astype(BF16)
        if h % 4 == 3:
            wide = slice((h - 3) * HEAD_DIM, (h + 1) * HEAD_DIM)
            for src, dst in ((dv, dv_hbm), (dq, dq_hbm), (dk, dk_hbm)):
                store(src.at[:, wide], dst.at[:, wide])
    for copy in stores:
        copy.wait()


VMEM = pl.BlockSpec(memory_space=pltpu.VMEM)
SMEM = pl.BlockSpec(memory_space=pltpu.SMEM)
ANY = pl.BlockSpec(memory_space=pl.ANY)


def shift(value, by):
    return lax.ppermute(value, "pool", [(i, (i + by) % RING) for i in range(RING)])


TOKEN = (COUNT, WIDTH)
CHUNK = (ROWS, WIDTH)
PAIR = (2 * ROWS, WIDTH)
SQUARES = (HEADS, COUNT, COUNT)
TABLE = (POOL, WIDTH)
OUTS = [
    (TOKEN, BF16, ANY), (TOKEN, BF16, ANY), (TOKEN, BF16, ANY), (TOKEN, BF16, ANY),
    ((XY, 1, WIDTH), F32, VMEM), (PAIR, BF16, ANY), (PAIR, BF16, ANY),
    (CHUNK, BF16, ANY), (CHUNK, BF16, ANY), (CHUNK, BF16, ANY), (CHUNK, BF16, ANY),
]
SCRATCH = [
    (TOKEN, BF16), (TOKEN, BF16), (TOKEN, BF16), (TOKEN, BF16), (TABLE, BF16),
    (SQUARES, BF16), (SQUARES, F32), ((COUNT, COUNT), F32), (TOKEN, F32), ((COUNT, HEAD_DIM), F32),
    (TOKEN, BF16), ((COUNT, POOL), F32), ((COUNT, POOL), BF16), (TABLE, BF16), (TOKEN, F32),
    (TOKEN, BF16), (TOKEN, BF16), (TOKEN, BF16), (TOKEN, BF16), (TOKEN, BF16),
]


def body(query_act, key_act, value_act, gate_act, lengths, targets, pool_rows, pool_ids, norm_gain):
    r2 = shift(pool_rows, 2)
    l2 = shift(pool_rows, -2)
    four = shift(pool_rows, 4)
    r1 = shift(pool_rows, 1)
    l1 = shift(pool_rows, -1)
    r3 = shift(r2, 1)
    l3 = shift(l2, -1)
    ids = lax.all_to_all(
        jnp.broadcast_to(pool_ids[None, None, :], (RING, 1, ROWS)), "pool", 0, 0, tiled=True
    ).reshape(1, POOL).astype(F32)
    place = lax.axis_index("pool").reshape(1).astype(I32)

    dq, dk, dv, gate_grad, part, plus1, minus1, plus4, plus2, minus2, kept = pl.pallas_call(
        step_kernel,
        out_shape=[jax.ShapeDtypeStruct(shape, kind) for shape, kind, _ in OUTS],
        in_specs=[SMEM, SMEM] + [ANY] * 4 + [VMEM] * 3 + [ANY] * 8,
        out_specs=[spec for _, _, spec in OUTS],
        scratch_shapes=[pltpu.VMEM(shape, kind) for shape, kind in SCRATCH]
        + [pltpu.SemaphoreType.DMA((12,)), pltpu.SemaphoreType.DMA((15,))],
        compiler_params=pltpu.CompilerParams(vmem_limit_bytes=LIMIT),
        cost_estimate=pl.CostEstimate(flops=2 * 10**9, bytes_accessed=8 * 10**6, transcendentals=720896),
    )(place, lengths, query_act, key_act, value_act, gate_act, norm_gain.reshape(1, WIDTH),
      targets.reshape(COUNT, 1), ids, pool_rows, r1, r2, r3, l1, l2, l3, four)

    from_left = shift(plus1, 1)
    from_right = shift(minus1, -1)
    from_far = shift(plus4, 4)

    plane = [[x * 16 + y * 2 + c for x in range(4) for y in range(8)] for c in range(2)]
    spread = lax.all_to_all(part, "dp", 0, 0, axis_index_groups=plane, tiled=True)
    spread = jnp.broadcast_to(jnp.sum(spread, axis=0, keepdims=True), (NEAR, 1, WIDTH))
    near = [[i * NEAR + j for j in range(NEAR)] for i in range(XY)]
    spread = lax.all_to_all(spread, ("dp", "pool"), 0, 0, axis_index_groups=near, tiled=True)
    gain_grad = jnp.sum(spread, axis=0).reshape(WIDTH)

    plus2 = (plus2.astype(F32) + from_left[:ROWS].astype(F32)).astype(BF16)
    minus2 = (minus2.astype(F32) + from_right[:ROWS].astype(F32)).astype(BF16)
    two_left = shift(plus2, 2)
    two_right = shift(minus2, -2)
    pool_grad = (
        kept.astype(F32) + from_left[ROWS:].astype(F32) + from_right[ROWS:].astype(F32)
        + from_far.astype(F32) + two_left.astype(F32) + two_right.astype(F32)
    )
    return (dq, dk, dv, gate_grad, pool_grad, gain_grad)


def solution(mesh):
    rows = P(("dp", "pool"), None)
    flat = P(("dp", "pool"))
    in_specs = (rows, rows, rows, rows, rows, flat, rows, flat, P())
    out_specs = (rows, rows, rows, rows, rows, P())
    return jax.shard_map(body, mesh=mesh, in_specs=in_specs, out_specs=out_specs, check_vma=False)
```

```python
import jax
import jax.numpy as jnp
from jax import lax
from jax.experimental import pallas as pl
from jax.experimental.pallas import tpu as pltpu
from jax.sharding import PartitionSpec as P

HEADS = 8
LMAX = 192
EPSILON = 1e-05
COUNT = 256
WIDTH = 1024
HEAD_DIM = 128
ROWS = 96
RING = 8
POOL = ROWS * RING
LIMIT = 56 * 1024 * 1024
EXTRA = 128
BASE = 64
XY = 32
NEAR = 16

F32 = jnp.float32
BF16 = jnp.bfloat16
I32 = jnp.int32
CONTRACT_LAST = (((1,), (1,)), ((), ()))
CONTRACT_FIRST = (((0,), (0,)), ((), ()))


def dot(a, b, dims=(((1,), (0,)), ((), ()))):
    return lax.dot_general(a, b, dims, preferred_element_type=F32)


def forward_kernel(
    lengths, q_hbm, k_hbm, v_hbm, gate_hbm, gain_ref, target_ref,
    emb_hbm, normed_hbm, aux_hbm, attend_hbm, slope_hbm,
    q, k, v, gate, emb, normed, aux, attend, slope, mask, came, went,
):
    loads = [
        pltpu.make_async_copy(src, dst, came.at[i])
        for i, (src, dst) in enumerate(((q_hbm, q), (k_hbm, k), (v_hbm, v), (gate_hbm, gate)))
    ]
    for load in loads:
        load.start()
    stores = []

    def store(src, dst):
        copy = pltpu.make_async_copy(src, dst, went.at[len(stores)])
        copy.start()
        stores.append(copy)

    scaling = HEAD_DIM ** (-0.5)
    row = lax.broadcasted_iota(I32, (COUNT, COUNT), 0)
    col = lax.broadcasted_iota(I32, (COUNT, COUNT), 1)
    first = jnp.zeros((COUNT, COUNT), I32)
    finish = jnp.int32(0)
    for i in range(lengths.shape[1]):
        finish = finish + lengths[0, i]
        first = jnp.where(row >= finish, finish, first)
    mask[...] = jnp.where((col >= first) & (col <= row), F32(1.0 / LMAX), F32(0.0))
    for load in loads[:3]:
        load.wait()
    for h in range(HEADS):
        lanes = slice(h * HEAD_DIM, (h + 1) * HEAD_DIM)
        scores = dot(q[:, lanes], k[:, lanes], CONTRACT_LAST) * scaling
        squash = 0.5 * jnp.tanh(0.5 * scores) + 0.5
        keep = mask[...]
        act = scores * squash
        weights = (act * keep).astype(BF16)
        attend[h] = weights
        slope[h] = (squash + act * (1.0 - squash)) * (keep * scaling)
        if h % 2 == 1:
            store(attend.at[h - 1 : h + 1], attend_hbm.at[h - 1 : h + 1])
            store(slope.at[h - 1 : h + 1], slope_hbm.at[h - 1 : h + 1])
        normed[:, lanes] = dot(weights, v[:, lanes])
    loads[3].wait()
    gain = gain_ref[...]
    step = 32
    for i in range(COUNT // step):
        at = slice(i * step, (i + 1) * step)
        part = normed[at, :]
        center = part - jnp.mean(part, axis=1, keepdims=True)
        scale = lax.rsqrt(jnp.mean(center * center, axis=1, keepdims=True) + EPSILON)
        unit = center * scale
        normed[at, :] = unit
        emb[at, :] = (unit * gain * gate[at, :].astype(F32)).astype(BF16)
        lane = lax.broadcasted_iota(I32, (step, HEAD_DIM), 1)
        token = lax.broadcasted_iota(I32, (step, HEAD_DIM), 0) + i * step
        usable = jnp.ones((step, HEAD_DIM), F32)
        finish = jnp.int32(0)
        for j in range(lengths.shape[1]):
            finish = finish + lengths[0, j]
            usable = jnp.where(token + 1 == finish, F32(0.0), usable)
        same = lax.broadcasted_iota(I32, (step, COUNT), 0) + i * step == lax.broadcasted_iota(I32, (step, COUNT), 1)
        target = jnp.sum(jnp.where(same, target_ref[...].astype(F32), F32(0.0)), axis=1, keepdims=True)
        aux[at, :] = jnp.where(lane == 0, scale, jnp.where(lane == 1, usable, target))
    store(emb, emb_hbm)
    store(normed, normed_hbm)
    store(aux, aux_hbm)
    for copy in stores:
        copy.wait()


def step_kernel(
    place, emb_hbm, normed_hbm, aux_hbm, attend_hbm, slope_hbm, q_hbm, k_hbm, v_hbm, gate_hbm, gain_ref,
    own, r1, r2, r3, r4, l1, l2, l3,
    dq_hbm, dk_hbm, dv_hbm, gate_grad_hbm, part_ref,
    plus1, minus1, plus4, plus2, minus2, kept,
    emb, rows, aux, normed, gate, q, k, v, attend, slope, logits, slopes, terms, back,
    dmixed, gate_grad, dq, dk, dv, came, went,
):
    z = place[0]
    ahead = place[1]

    def start_of(offset):
        return pl.multiple_of(lax.rem(z + ahead * offset + RING, RING) * ROWS, 16)

    stores = []

    def store(src, dst):
        copy = pltpu.make_async_copy(src, dst, went.at[len(stores)])
        copy.start()
        stores.append(copy)

    pairs = [(emb_hbm, emb)]
    for offset, ref in ((0, own), (-1, r1), (-2, r2), (-3, r3), (-4, r4), (1, l1), (2, l2), (3, l3)):
        pairs.append((ref, rows.at[pl.ds(start_of(offset), ROWS), :]))
    pairs += [(aux_hbm, aux), (normed_hbm, normed), (gate_hbm, gate)]
    pairs += [(v_hbm, v), (slope_hbm, slope), (attend_hbm, attend), (k_hbm, k), (q_hbm, q)]
    loads = [pltpu.make_async_copy(src, dst, came.at[i]) for i, (src, dst) in enumerate(pairs)]
    for load in loads:
        load.start()
    for load in loads[:10]:
        load.wait()

    logits[...] = dot(emb[...], rows[:, 0:WIDTH], CONTRACT_LAST)
    lane = lax.broadcasted_iota(I32, (8, EXTRA), 1)
    digits = jnp.where(lane == 0, F32(BASE), jnp.where(lane == 1, F32(1.0), F32(0.0))).astype(BF16)
    ids = dot(digits, rows[:, WIDTH : WIDTH + EXTRA], CONTRACT_LAST)[0:1, :]
    step = 32
    for i in range(COUNT // step):
        at = slice(i * step, (i + 1) * step)
        column = lax.broadcasted_iota(I32, (step, POOL), 1).astype(F32)
        chosen = column == aux[at, 2:3]
        own_id = jnp.sum(jnp.where(chosen, ids, F32(0.0)), axis=1, keepdims=True)
        clash = (ids == own_id) & jnp.logical_not(chosen)
        masked = jnp.where(clash, F32(-1e30), logits[at, :])
        peak = jnp.max(masked, axis=1, keepdims=True)
        weight = jnp.where(clash, F32(0.0), jnp.exp(masked - peak))
        total = jnp.sum(weight, axis=1, keepdims=True)
        probs = weight * (1.0 / total)
        slopes[at, :] = (aux[at, 1:2] * jnp.where(chosen, probs - 1.0, probs)).astype(BF16)

    terms[...] = dot(slopes[...], emb[...], CONTRACT_FIRST).astype(BF16)
    for offset, ref in (
        (3, plus1.at[0:ROWS]), (1, plus1.at[ROWS : 2 * ROWS]),
        (-3, minus1.at[0:ROWS]), (-1, minus1.at[ROWS : 2 * ROWS]),
        (4, plus4), (2, plus2), (-2, minus2), (0, kept),
    ):
        store(terms.at[pl.ds(start_of(offset), ROWS), :], ref)

    back[...] = dot(slopes[...], rows[:, 0:WIDTH])
    for load in loads[10:12]:
        load.wait()
    gain = gain_ref[...]
    sums = jnp.zeros((8, WIDTH), F32)
    for i in range(COUNT // step):
        at = slice(i * step, (i + 1) * step)
        unit = normed[at, :]
        pulled = back[at, :]
        gate_grad[at, :] = (pulled * (unit * gain)).astype(BF16)
        dscaled = pulled * gate[at, :].astype(F32)
        product = dscaled * unit
        sums = sums + jnp.sum(product.reshape(step // 8, 8, WIDTH), axis=0)
        dnormed = dscaled * gain
        mean1 = jnp.mean(dnormed, axis=1, keepdims=True)
        mean2 = jnp.mean(product * gain, axis=1, keepdims=True)
        dmixed[at, :] = ((dnormed - mean1 - unit * mean2) * aux[at, 0:1]).astype(BF16)
    store(gate_grad, gate_grad_hbm)
    part = jnp.sum(sums, axis=0, keepdims=True)
    for i in range(XY):
        part_ref[i] = part

    for load in loads[12:]:
        load.wait()
    for h in range(HEADS):
        lanes = slice(h * HEAD_DIM, (h + 1) * HEAD_DIM)
        part = dmixed[:, lanes]
        dattend = dot(part, v[:, lanes], CONTRACT_LAST)
        dscores = (dattend * slope[h]).astype(BF16)
        dv[:, lanes] = dot(attend[h], part, CONTRACT_FIRST).astype(BF16)
        dq[:, lanes] = dot(dscores, k[:, lanes]).astype(BF16)
        dk[:, lanes] = dot(dscores, q[:, lanes], CONTRACT_FIRST).astype(BF16)
        if h % 2 == 1:
            wide = slice((h - 1) * HEAD_DIM, (h + 1) * HEAD_DIM)
            for src, dst in ((dv, dv_hbm), (dq, dq_hbm), (dk, dk_hbm)):
                store(src.at[:, wide], dst.at[:, wide])
    for copy in stores:
        copy.wait()


VMEM = pl.BlockSpec(memory_space=pltpu.VMEM)
SMEM = pl.BlockSpec(memory_space=pltpu.SMEM)
ANY = pl.BlockSpec(memory_space=pl.ANY)


def call(kernel, specs, outs, scratch, copies, cost):
    return pl.pallas_call(
        kernel,
        out_shape=[jax.ShapeDtypeStruct(shape, kind) for shape, kind, _ in outs],
        in_specs=specs,
        out_specs=[spec for _, _, spec in outs],
        scratch_shapes=[pltpu.VMEM(shape, kind) for shape, kind in scratch]
        + [pltpu.SemaphoreType.DMA((count,)) for count in copies],
        compiler_params=pltpu.CompilerParams(vmem_limit_bytes=LIMIT),
        cost_estimate=pl.CostEstimate(flops=cost, bytes_accessed=8 * 10**6, transcendentals=524288),
    )


def shift(value, by):
    pairs = []
    for line in range(2 * XY):
        ahead = by if line % 2 == 0 else -by
        pairs += [(line * RING + i, line * RING + (i + ahead) % RING) for i in range(RING)]
    return lax.ppermute(value, ("dp", "pool"), pairs)


TOKEN = (COUNT, WIDTH)
CHUNK = (ROWS, WIDTH)
PAIR = (2 * ROWS, WIDTH)
SQUARES = (HEADS, COUNT, COUNT)
LANES = (COUNT, HEAD_DIM)
TABLE = (POOL, WIDTH)


def body(query_act, key_act, value_act, gate_act, lengths, targets, pool_rows, pool_ids, norm_gain):
    lane = lax.broadcasted_iota(I32, (ROWS, EXTRA), 1)
    column = pool_ids[:, None]
    digits = jnp.where(lane == 0, column // BASE, jnp.where(lane == 1, column % BASE, 0))
    mine = jnp.concatenate([pool_rows, digits.astype(BF16)], axis=1)
    r2 = shift(mine, 2)
    l2 = shift(mine, -2)
    r1 = shift(mine, 1)
    l1 = shift(mine, -1)
    r4 = shift(r2, 2)
    r3 = shift(r2, 1)
    l3 = shift(l2, -1)
    core = lax.rem(lax.axis_index("dp"), 2)
    place = jnp.stack([lax.axis_index("pool"), 1 - 2 * core]).astype(I32)
    gain = norm_gain.reshape(1, WIDTH)

    emb, normed, aux, attend, slope = call(
        forward_kernel,
        [SMEM] + [ANY] * 4 + [VMEM] * 2,
        [(TOKEN, BF16, ANY), (TOKEN, F32, ANY), (LANES, F32, ANY), (SQUARES, BF16, ANY), (SQUARES, F32, ANY)],
        [(TOKEN, BF16)] * 5 + [(TOKEN, F32), (LANES, F32), (SQUARES, BF16), (SQUARES, F32), ((COUNT, COUNT), F32)],
        (4, HEADS + 3),
        10**9,
    )(lengths, query_act, key_act, value_act, gate_act, gain, targets.reshape(1, COUNT))

    dq, dk, dv, gate_grad, part, plus1, minus1, plus4, plus2, minus2, kept = call(
        step_kernel,
        [SMEM] + [ANY] * 9 + [VMEM] + [ANY] * 8,
        [(TOKEN, BF16, ANY)] * 4
        + [((XY, 1, WIDTH), F32, VMEM), (PAIR, BF16, ANY), (PAIR, BF16, ANY)]
        + [(CHUNK, BF16, ANY)] * 4,
        [(TOKEN, BF16), ((POOL, WIDTH + EXTRA), BF16), (LANES, F32), (TOKEN, F32)]
        + [(TOKEN, BF16)] * 4
        + [(SQUARES, BF16), (SQUARES, F32), ((COUNT, POOL), F32), ((COUNT, POOL), BF16), (TABLE, BF16), (TOKEN, F32)]
        + [(TOKEN, BF16)] * 5,
        (17, 21),
        2 * 10**9,
    )(place, emb, normed, aux, attend, slope, query_act, key_act, value_act, gate_act, gain,
      mine, r1, r2, r3, r4, l1, l2, l3)

    from_left = shift(plus1, 1)
    from_right = shift(minus1, -1)
    from_far = shift(plus4, 2)
    from_left, from_right, from_far = lax.optimization_barrier((from_left, from_right, from_far))
    plus2 = (plus2.astype(F32) + from_left[:ROWS].astype(F32) + from_far.astype(F32)).astype(BF16)
    minus2 = (minus2.astype(F32) + from_right[:ROWS].astype(F32)).astype(BF16)
    two_left = shift(plus2, 2)
    two_right = shift(minus2, -2)

    plane = [[x * 16 + y * 2 + c for x in range(4) for y in range(8)] for c in range(2)]
    spread = lax.all_to_all(part, "dp", 0, 0, axis_index_groups=plane, tiled=True)
    spread = jnp.broadcast_to(jnp.sum(spread, axis=0, keepdims=True), (NEAR, 1, WIDTH))
    near = [[i * NEAR + j for j in range(NEAR)] for i in range(XY)]
    spread = lax.all_to_all(spread, ("dp", "pool"), 0, 0, axis_index_groups=near, tiled=True)
    gain_grad = jnp.sum(spread, axis=0).reshape(WIDTH)

    pool_grad = (
        kept.astype(F32) + from_left[ROWS:].astype(F32) + from_right[ROWS:].astype(F32)
        + two_left.astype(F32) + two_right.astype(F32)
    )
    return (dq, dk, dv, gate_grad, pool_grad, gain_grad)


def solution(mesh):
    rows = P(("dp", "pool"), None)
    flat = P(("dp", "pool"))
    in_specs = (rows, rows, rows, rows, rows, flat, rows, flat, P())
    out_specs = (rows, rows, rows, rows, rows, P())
    return jax.shard_map(body, mesh=mesh, in_specs=in_specs, out_specs=out_specs, check_vma=False)
```

```python
import jax
import jax.numpy as jnp
from jax import lax
from jax.experimental import pallas as pl
from jax.experimental.pallas import tpu as pltpu
from jax.sharding import PartitionSpec as P

HEADS = 8
LMAX = 192
EPSILON = 1e-05
COUNT = 256
WIDTH = 1024
HEAD_DIM = 128
ROWS = 96
RING = 8
POOL = ROWS * RING
LIMIT = 56 * 1024 * 1024
EXTRA = 128
BASE = 64
XY = 32
NEAR = 16

F32 = jnp.float32
BF16 = jnp.bfloat16
I32 = jnp.int32
CONTRACT_LAST = (((1,), (1,)), ((), ()))
CONTRACT_FIRST = (((0,), (0,)), ((), ()))


def dot(a, b, dims=(((1,), (0,)), ((), ()))):
    return lax.dot_general(a, b, dims, preferred_element_type=F32)


def forward_kernel(
    lengths, q_hbm, k_hbm, v_hbm, gate_hbm, gain_ref, target_ref,
    emb_hbm, normed_hbm, aux_hbm, attend_hbm, slope_hbm,
    q, k, v, gate, emb, normed, aux, attend, slope, mask, came, went,
):
    halves = (slice(0, WIDTH // 2), slice(WIDTH // 2, WIDTH))
    pairs = [
        (src.at[:, half], dst.at[:, half])
        for half in halves
        for src, dst in ((q_hbm, q), (k_hbm, k), (v_hbm, v))
    ] + [(gate_hbm, gate)]
    loads = [pltpu.make_async_copy(src, dst, came.at[i]) for i, (src, dst) in enumerate(pairs)]
    for load in loads:
        load.start()
    stores = []

    def store(src, dst):
        copy = pltpu.make_async_copy(src, dst, went.at[len(stores)])
        copy.start()
        stores.append(copy)

    scaling = HEAD_DIM ** (-0.5)
    row = lax.broadcasted_iota(I32, (COUNT, COUNT), 0)
    col = lax.broadcasted_iota(I32, (COUNT, COUNT), 1)
    first = jnp.zeros((COUNT, COUNT), I32)
    finish = jnp.int32(0)
    for i in range(lengths.shape[1]):
        finish = finish + lengths[0, i]
        first = jnp.where(row >= finish, finish, first)
    mask[...] = jnp.where((col >= first) & (col <= row), F32(1.0 / LMAX), F32(0.0))
    for h in range(HEADS):
        if h % 4 == 0:
            for load in loads[h // 4 * 3 : h // 4 * 3 + 3]:
                load.wait()
        lanes = slice(h * HEAD_DIM, (h + 1) * HEAD_DIM)
        scores = dot(q[:, lanes], k[:, lanes], CONTRACT_LAST) * scaling
        squash = 0.5 * jnp.tanh(0.5 * scores) + 0.5
        keep = mask[...]
        act = scores * squash
        weights = (act * keep).astype(BF16)
        attend[h] = weights
        slope[h] = (squash + act * (1.0 - squash)) * (keep * scaling)
        if h % 2 == 1:
            store(attend.at[h - 1 : h + 1], attend_hbm.at[h - 1 : h + 1])
            store(slope.at[h - 1 : h + 1], slope_hbm.at[h - 1 : h + 1])
        normed[:, lanes] = dot(weights, v[:, lanes])
    loads[6].wait()
    gain = gain_ref[...]
    step = 32
    for i in range(COUNT // step):
        at = slice(i * step, (i + 1) * step)
        part = normed[at, :]
        center = part - jnp.mean(part, axis=1, keepdims=True)
        scale = lax.rsqrt(jnp.mean(center * center, axis=1, keepdims=True) + EPSILON)
        unit = center * scale
        normed[at, :] = unit
        emb[at, :] = (unit * gain * gate[at, :].astype(F32)).astype(BF16)
        lane = lax.broadcasted_iota(I32, (step, HEAD_DIM), 1)
        token = lax.broadcasted_iota(I32, (step, HEAD_DIM), 0) + i * step
        usable = jnp.ones((step, HEAD_DIM), F32)
        finish = jnp.int32(0)
        for j in range(lengths.shape[1]):
            finish = finish + lengths[0, j]
            usable = jnp.where(token + 1 == finish, F32(0.0), usable)
        same = lax.broadcasted_iota(I32, (step, COUNT), 0) + i * step == lax.broadcasted_iota(I32, (step, COUNT), 1)
        target = jnp.sum(jnp.where(same, target_ref[...].astype(F32), F32(0.0)), axis=1, keepdims=True)
        aux[at, :] = jnp.where(lane == 0, scale, jnp.where(lane == 1, usable, target))
        if i % 4 == 3:
            half = slice((i - 3) * step, (i + 1) * step)
            store(normed.at[half], normed_hbm.at[half])
            store(emb.at[half], emb_hbm.at[half])
    store(aux, aux_hbm)
    for copy in stores:
        copy.wait()


def step_kernel(
    place, line, emb_hbm, normed_hbm, aux_hbm, gate_hbm, gain_ref,
    own, r1, r2, r3, l1, l2, l3, l4,
    gate_grad_hbm, dmixed_hbm, part_ref,
    plus1, minus1, plus4, plus2, minus2, kept,
    emb, rows, aux, normed, gate, logits, slopes, terms, back, dmixed, gate_grad, came, went,
):
    z = place[0]
    ahead = 1 - 2 * lax.rem(line[0], 2)

    def start_of(offset):
        return pl.multiple_of(lax.rem(z + ahead * offset + RING, RING) * ROWS, 16)

    stores = []

    def store(src, dst):
        copy = pltpu.make_async_copy(src, dst, went.at[len(stores)])
        copy.start()
        stores.append(copy)

    pairs = [(emb_hbm, emb)]
    for offset, ref in ((0, own), (-1, r1), (-2, r2), (-3, r3), (1, l1), (2, l2), (3, l3), (4, l4)):
        pairs.append((ref, rows.at[pl.ds(start_of(offset), ROWS), :]))
    pairs += [(aux_hbm, aux), (normed_hbm, normed), (gate_hbm, gate)]
    loads = [pltpu.make_async_copy(src, dst, came.at[i]) for i, (src, dst) in enumerate(pairs)]
    for load in loads:
        load.start()
    for load in loads[:10]:
        load.wait()

    logits[...] = dot(emb[...], rows[:, 0:WIDTH], CONTRACT_LAST)
    lane = lax.broadcasted_iota(I32, (8, EXTRA), 1)
    digits = jnp.where(lane == 0, F32(BASE), jnp.where(lane == 1, F32(1.0), F32(0.0))).astype(BF16)
    ids = dot(digits, rows[:, WIDTH : WIDTH + EXTRA], CONTRACT_LAST)[0:1, :]
    step = 32
    for i in range(COUNT // step):
        at = slice(i * step, (i + 1) * step)
        column = lax.broadcasted_iota(I32, (step, POOL), 1).astype(F32)
        chosen = column == aux[at, 2:3]
        own_id = jnp.sum(jnp.where(chosen, ids, F32(0.0)), axis=1, keepdims=True)
        clash = (ids == own_id) & jnp.logical_not(chosen)
        masked = jnp.where(clash, F32(-1e30), logits[at, :])
        peak = jnp.max(masked, axis=1, keepdims=True)
        weight = jnp.where(clash, F32(0.0), jnp.exp(masked - peak))
        total = jnp.sum(weight, axis=1, keepdims=True)
        probs = weight * (1.0 / total)
        slopes[at, :] = (aux[at, 1:2] * jnp.where(chosen, probs - 1.0, probs)).astype(BF16)

    terms[...] = dot(slopes[...], emb[...], CONTRACT_FIRST).astype(BF16)
    for offset, ref in (
        (3, plus1.at[0:ROWS]), (1, plus1.at[ROWS : 2 * ROWS]),
        (-3, minus1.at[0:ROWS]), (-1, minus1.at[ROWS : 2 * ROWS]),
        (4, plus4), (2, plus2), (-2, minus2), (0, kept),
    ):
        store(terms.at[pl.ds(start_of(offset), ROWS), :], ref)

    back[...] = dot(slopes[...], rows[:, 0:WIDTH])
    for load in loads[10:12]:
        load.wait()
    gain = gain_ref[...]
    sums = jnp.zeros((8, WIDTH), F32)
    for i in range(COUNT // step):
        at = slice(i * step, (i + 1) * step)
        unit = normed[at, :]
        pulled = back[at, :]
        gate_grad[at, :] = (pulled * (unit * gain)).astype(BF16)
        dscaled = pulled * gate[at, :].astype(F32)
        product = dscaled * unit
        sums = sums + jnp.sum(product.reshape(step // 8, 8, WIDTH), axis=0)
        dnormed = dscaled * gain
        mean1 = jnp.mean(dnormed, axis=1, keepdims=True)
        mean2 = jnp.mean(product * gain, axis=1, keepdims=True)
        dmixed[at, :] = ((dnormed - mean1 - unit * mean2) * aux[at, 0:1]).astype(BF16)
    store(dmixed, dmixed_hbm)
    store(gate_grad, gate_grad_hbm)
    part = jnp.sum(sums, axis=0, keepdims=True)
    for i in range(XY):
        part_ref[i] = part

    for copy in stores:
        copy.wait()


def backward_kernel(
    dmixed_hbm, q_hbm, k_hbm, v_hbm, attend_hbm, slope_hbm, dq_hbm, dk_hbm, dv_hbm,
    dmixed, q, k, v, attend, slope, dq, dk, dv, came, went,
):
    pairs = []
    for half in range(2):
        lanes = slice(half * WIDTH // 2, (half + 1) * WIDTH // 2)
        heads = slice(half * HEADS // 2, (half + 1) * HEADS // 2)
        pairs += [(src.at[:, lanes], dst.at[:, lanes]) for src, dst in ((dmixed_hbm, dmixed), (v_hbm, v))]
        pairs += [(src.at[heads], dst.at[heads]) for src, dst in ((slope_hbm, slope), (attend_hbm, attend))]
        pairs += [(src.at[:, lanes], dst.at[:, lanes]) for src, dst in ((k_hbm, k), (q_hbm, q))]
    loads = [pltpu.make_async_copy(src, dst, came.at[i]) for i, (src, dst) in enumerate(pairs)]
    for load in loads:
        load.start()
    stores = []
    for h in range(HEADS):
        if h % 4 == 0:
            for load in loads[h // 4 * 6 : h // 4 * 6 + 6]:
                load.wait()
        lanes = slice(h * HEAD_DIM, (h + 1) * HEAD_DIM)
        part = dmixed[:, lanes]
        dattend = dot(part, v[:, lanes], CONTRACT_LAST)
        dscores = (dattend * slope[h]).astype(BF16)
        dv[:, lanes] = dot(attend[h], part, CONTRACT_FIRST).astype(BF16)
        dq[:, lanes] = dot(dscores, k[:, lanes]).astype(BF16)
        dk[:, lanes] = dot(dscores, q[:, lanes], CONTRACT_FIRST).astype(BF16)
        if h % 2 == 1:
            wide = slice((h - 1) * HEAD_DIM, (h + 1) * HEAD_DIM)
            for src, dst in ((dv, dv_hbm), (dq, dq_hbm), (dk, dk_hbm)):
                copy = pltpu.make_async_copy(src.at[:, wide], dst.at[:, wide], went.at[len(stores)])
                copy.start()
                stores.append(copy)
    for copy in stores:
        copy.wait()


VMEM = pl.BlockSpec(memory_space=pltpu.VMEM)
SMEM = pl.BlockSpec(memory_space=pltpu.SMEM)
ANY = pl.BlockSpec(memory_space=pl.ANY)


def call(kernel, specs, outs, scratch, copies, cost, limit=LIMIT):
    return pl.pallas_call(
        kernel,
        out_shape=[jax.ShapeDtypeStruct(shape, kind) for shape, kind, _ in outs],
        in_specs=specs,
        out_specs=[spec for _, _, spec in outs],
        scratch_shapes=[pltpu.VMEM(shape, kind) for shape, kind in scratch]
        + [pltpu.SemaphoreType.DMA((count,)) for count in copies],
        compiler_params=pltpu.CompilerParams(vmem_limit_bytes=limit),
        cost_estimate=pl.CostEstimate(flops=cost, bytes_accessed=8 * 10**6, transcendentals=524288),
    )


def shift(value, by):
    pairs = []
    for line in range(2 * XY):
        ahead = by if line % 2 == 0 else -by
        pairs += [(line * RING + i, line * RING + (i + ahead) % RING) for i in range(RING)]
    return lax.ppermute(value, ("dp", "pool"), pairs)


TOKEN = (COUNT, WIDTH)
CHUNK = (ROWS, WIDTH)
PAIR = (2 * ROWS, WIDTH)
SQUARES = (HEADS, COUNT, COUNT)
LANES = (COUNT, HEAD_DIM)
TABLE = (POOL, WIDTH)


def body(query_act, key_act, value_act, gate_act, lengths, targets, pool_rows, pool_ids, norm_gain):
    lane = lax.broadcasted_iota(I32, (ROWS, EXTRA), 1)
    column = pool_ids[:, None]
    digits = jnp.where(lane == 0, column // BASE, jnp.where(lane == 1, column % BASE, 0))
    mine = jnp.concatenate([pool_rows, digits.astype(BF16)], axis=1)
    r2 = shift(mine, 2)
    l2 = shift(mine, -2)
    r1 = shift(mine, 1)
    l1 = shift(mine, -1)
    l4 = shift(l2, -2)
    r3 = shift(r2, 1)
    l3 = shift(l2, -1)
    place = lax.axis_index("pool").reshape(1).astype(I32)
    line = lax.axis_index("dp").reshape(1).astype(I32)
    gain = norm_gain.reshape(1, WIDTH)

    emb, normed, aux, attend, slope = call(
        forward_kernel,
        [SMEM] + [ANY] * 4 + [VMEM] * 2,
        [(TOKEN, BF16, ANY), (TOKEN, F32, ANY), (LANES, F32, ANY), (SQUARES, BF16, ANY), (SQUARES, F32, ANY)],
        [(TOKEN, BF16)] * 5 + [(TOKEN, F32), (LANES, F32), (SQUARES, BF16), (SQUARES, F32), ((COUNT, COUNT), F32)],
        (7, HEADS + 5),
        10**9,
    )(lengths, query_act, key_act, value_act, gate_act, gain, targets.reshape(1, COUNT))

    gate_grad, dmixed, part, plus1, minus1, plus4, plus2, minus2, kept = call(
        step_kernel,
        [SMEM, SMEM] + [ANY] * 4 + [VMEM] + [ANY] * 8,
        [(TOKEN, BF16, ANY)] * 2
        + [((XY, 1, WIDTH), F32, VMEM), (PAIR, BF16, ANY), (PAIR, BF16, ANY)]
        + [(CHUNK, BF16, ANY)] * 4,
        [(TOKEN, BF16), ((POOL, WIDTH + EXTRA), BF16), (LANES, F32), (TOKEN, F32), (TOKEN, BF16)]
        + [((COUNT, POOL), F32), ((COUNT, POOL), BF16), (TABLE, BF16), (TOKEN, F32)]
        + [(TOKEN, BF16)] * 2,
        (12, 10),
        2 * 10**9,
    )(place, line, emb, normed, aux, gate_act, gain, mine, r1, r2, r3, l1, l2, l3, l4)

    from_left = shift(plus1, 1)
    from_right = shift(minus1, -1)
    from_far = shift(plus4, 2)
    from_left, from_right, from_far = lax.optimization_barrier((from_left, from_right, from_far))
    plus2 = (plus2.astype(F32) + from_left[:ROWS].astype(F32) + from_far.astype(F32)).astype(BF16)
    minus2 = (minus2.astype(F32) + from_right[:ROWS].astype(F32)).astype(BF16)
    two_left = shift(plus2, 2)
    two_right = shift(minus2, -2)

    plane = [[x * 16 + y * 2 + c for x in range(4) for y in range(8)] for c in range(2)]
    spread = lax.all_to_all(part, "dp", 0, 0, axis_index_groups=plane, tiled=True)
    spread = jnp.broadcast_to(jnp.sum(spread, axis=0, keepdims=True), (NEAR, 1, WIDTH))
    near = [[i * NEAR + j for j in range(NEAR)] for i in range(XY)]
    spread = lax.all_to_all(spread, ("dp", "pool"), 0, 0, axis_index_groups=near, tiled=True)
    gain_grad = jnp.sum(spread, axis=0).reshape(WIDTH)

    pool_grad = (
        kept.astype(F32) + from_left[ROWS:].astype(F32) + from_right[ROWS:].astype(F32)
        + two_left.astype(F32) + two_right.astype(F32)
    )
    dq, dk, dv = call(
        backward_kernel,
        [ANY] * 6,
        [(TOKEN, BF16, ANY)] * 3,
        [(TOKEN, BF16)] * 4 + [(SQUARES, BF16), (SQUARES, F32)] + [(TOKEN, BF16)] * 3,
        (12, 12),
        2 * 10**9,
    )(dmixed, query_act, key_act, value_act, attend, slope)
    return (dq, dk, dv, gate_grad, pool_grad, gain_grad)


def solution(mesh):
    rows = P(("dp", "pool"), None)
    flat = P(("dp", "pool"))
    in_specs = (rows, rows, rows, rows, rows, flat, rows, flat, P())
    out_specs = (rows, rows, rows, rows, rows, P())
    return jax.shard_map(body, mesh=mesh, in_specs=in_specs, out_specs=out_specs, check_vma=False)
```

```python
import jax
import jax.numpy as jnp
from jax import lax
from jax.experimental import pallas as pl
from jax.experimental.pallas import tpu as pltpu
from jax.sharding import PartitionSpec as P

HEADS = 8
LMAX = 192
EPSILON = 1e-05
COUNT = 256
WIDTH = 1024
HEAD_DIM = 128
ROWS = 96
RING = 8
POOL = ROWS * RING
LIMIT = 56 * 1024 * 1024
EXTRA = 128
BASE = 64
XY = 32
NEAR = 16

F32 = jnp.float32
BF16 = jnp.bfloat16
I32 = jnp.int32
CONTRACT_LAST = (((1,), (1,)), ((), ()))
CONTRACT_FIRST = (((0,), (0,)), ((), ()))


def dot(a, b, dims=(((1,), (0,)), ((), ()))):
    return lax.dot_general(a, b, dims, preferred_element_type=F32)


def forward_kernel(
    lengths, q_hbm, k_hbm, v_hbm, gate_hbm, gain_ref, target_ref,
    emb_hbm, normed_hbm, aux_hbm, attend_hbm, slope_hbm,
    q, k, v, gate, emb, normed, aux, attend, slope, mask, came, went,
):
    halves = (slice(0, WIDTH // 2), slice(WIDTH // 2, WIDTH))
    pairs = [
        (src.at[:, half], dst.at[:, half])
        for half in halves
        for src, dst in ((q_hbm, q), (k_hbm, k), (v_hbm, v))
    ] + [(gate_hbm, gate)]
    loads = [pltpu.make_async_copy(src, dst, came.at[i]) for i, (src, dst) in enumerate(pairs)]
    for load in loads:
        load.start()
    stores = []

    def store(src, dst):
        copy = pltpu.make_async_copy(src, dst, went.at[len(stores)])
        copy.start()
        stores.append(copy)

    scaling = HEAD_DIM ** (-0.5)
    row = lax.broadcasted_iota(I32, (COUNT, COUNT), 0)
    col = lax.broadcasted_iota(I32, (COUNT, COUNT), 1)
    first = jnp.zeros((COUNT, COUNT), I32)
    finish = jnp.int32(0)
    for i in range(lengths.shape[1]):
        finish = finish + lengths[0, i]
        first = jnp.where(row >= finish, finish, first)
    mask[...] = jnp.where((col >= first) & (col <= row), F32(1.0 / LMAX), F32(0.0))
    for h in range(HEADS):
        if h % 4 == 0:
            for load in loads[h // 4 * 3 : h // 4 * 3 + 3]:
                load.wait()
        lanes = slice(h * HEAD_DIM, (h + 1) * HEAD_DIM)
        scores = dot(q[:, lanes], k[:, lanes], CONTRACT_LAST) * scaling
        squash = 0.5 * jnp.tanh(0.5 * scores) + 0.5
        keep = mask[...]
        act = scores * squash
        weights = (act * keep).astype(BF16)
        attend[h] = weights
        slope[h] = (squash + act * (1.0 - squash)) * (keep * scaling)
        if h % 2 == 1:
            store(attend.at[h - 1 : h + 1], attend_hbm.at[h - 1 : h + 1])
            store(slope.at[h - 1 : h + 1], slope_hbm.at[h - 1 : h + 1])
        normed[:, lanes] = dot(weights, v[:, lanes])
    loads[6].wait()
    gain = gain_ref[...]
    step = 32
    for i in range(COUNT // step):
        at = slice(i * step, (i + 1) * step)
        part = normed[at, :]
        center = part - jnp.mean(part, axis=1, keepdims=True)
        scale = lax.rsqrt(jnp.mean(center * center, axis=1, keepdims=True) + EPSILON)
        unit = center * scale
        normed[at, :] = unit
        emb[at, :] = (unit * gain * gate[at, :].astype(F32)).astype(BF16)
        lane = lax.broadcasted_iota(I32, (step, HEAD_DIM), 1)
        token = lax.broadcasted_iota(I32, (step, HEAD_DIM), 0) + i * step
        usable = jnp.ones((step, HEAD_DIM), F32)
        finish = jnp.int32(0)
        for j in range(lengths.shape[1]):
            finish = finish + lengths[0, j]
            usable = jnp.where(token + 1 == finish, F32(0.0), usable)
        same = lax.broadcasted_iota(I32, (step, COUNT), 0) + i * step == lax.broadcasted_iota(I32, (step, COUNT), 1)
        target = jnp.sum(jnp.where(same, target_ref[...].astype(F32), F32(0.0)), axis=1, keepdims=True)
        aux[at, :] = jnp.where(lane == 0, scale, jnp.where(lane == 1, usable, target))
        if i % 4 == 3:
            half = slice((i - 3) * step, (i + 1) * step)
            store(normed.at[half], normed_hbm.at[half])
            store(emb.at[half], emb_hbm.at[half])
    store(aux, aux_hbm)
    for copy in stores:
        copy.wait()


def step_kernel(
    place, line, emb_hbm, normed_hbm, aux_hbm, gate_hbm, gain_ref,
    own, r1, r2, r3, l1, l2, l3, l4,
    gate_grad_hbm, dmixed_hbm, part_ref,
    plus1, minus1, plus4, plus2, minus2, kept,
    emb, rows, aux, normed, gate, logits, slopes, terms, back, dmixed, gate_grad, came, went,
):
    z = place[0]
    ahead = 1 - 2 * lax.rem(line[0], 2)

    def start_of(offset):
        return pl.multiple_of(lax.rem(z + ahead * offset + RING, RING) * ROWS, 16)

    stores = []

    def store(src, dst):
        copy = pltpu.make_async_copy(src, dst, went.at[len(stores)])
        copy.start()
        stores.append(copy)

    pairs = [(emb_hbm, emb)]
    for offset, ref in ((0, own), (-1, r1), (-2, r2), (-3, r3), (1, l1), (2, l2), (3, l3), (4, l4)):
        pairs.append((ref, rows.at[pl.ds(start_of(offset), ROWS), :]))
    pairs += [(aux_hbm, aux), (normed_hbm, normed), (gate_hbm, gate)]
    loads = [pltpu.make_async_copy(src, dst, came.at[i]) for i, (src, dst) in enumerate(pairs)]
    for load in loads:
        load.start()
    for load in loads[:10]:
        load.wait()

    logits[...] = dot(emb[...], rows[:, 0:WIDTH], CONTRACT_LAST)
    lane = lax.broadcasted_iota(I32, (8, EXTRA), 1)
    digits = jnp.where(lane == 0, F32(BASE), jnp.where(lane == 1, F32(1.0), F32(0.0))).astype(BF16)
    ids = dot(digits, rows[:, WIDTH : WIDTH + EXTRA], CONTRACT_LAST)[0:1, :]
    step = 32
    for i in range(COUNT // step):
        at = slice(i * step, (i + 1) * step)
        column = lax.broadcasted_iota(I32, (step, POOL), 1).astype(F32)
        chosen = column == aux[at, 2:3]
        own_id = jnp.sum(jnp.where(chosen, ids, F32(0.0)), axis=1, keepdims=True)
        clash = (ids == own_id) & jnp.logical_not(chosen)
        masked = jnp.where(clash, F32(-1e30), logits[at, :])
        peak = jnp.max(masked, axis=1, keepdims=True)
        weight = jnp.where(clash, F32(0.0), jnp.exp(masked - peak))
        total = jnp.sum(weight, axis=1, keepdims=True)
        probs = weight * (1.0 / total)
        slopes[at, :] = (aux[at, 1:2] * jnp.where(chosen, probs - 1.0, probs)).astype(BF16)

    terms[...] = dot(slopes[...], emb[...], CONTRACT_FIRST).astype(BF16)
    for offset, ref in (
        (3, plus1.at[0:ROWS]), (1, plus1.at[ROWS : 2 * ROWS]),
        (-3, minus1.at[0:ROWS]), (-1, minus1.at[ROWS : 2 * ROWS]),
        (4, plus4), (2, plus2), (-2, minus2), (0, kept),
    ):
        store(terms.at[pl.ds(start_of(offset), ROWS), :], ref)

    back[...] = dot(slopes[...], rows[:, 0:WIDTH])
    for load in loads[10:12]:
        load.wait()
    gain = gain_ref[...]
    sums = jnp.zeros((8, WIDTH), F32)
    for i in range(COUNT // step):
        at = slice(i * step, (i + 1) * step)
        unit = normed[at, :]
        pulled = back[at, :]
        gate_grad[at, :] = (pulled * (unit * gain)).astype(BF16)
        dscaled = pulled * gate[at, :].astype(F32)
        product = dscaled * unit
        sums = sums + jnp.sum(product.reshape(step // 8, 8, WIDTH), axis=0)
        dnormed = dscaled * gain
        mean1 = jnp.mean(dnormed, axis=1, keepdims=True)
        mean2 = jnp.mean(product * gain, axis=1, keepdims=True)
        dmixed[at, :] = ((dnormed - mean1 - unit * mean2) * aux[at, 0:1]).astype(BF16)
    store(dmixed, dmixed_hbm)
    store(gate_grad, gate_grad_hbm)
    part = jnp.sum(sums, axis=0, keepdims=True)
    for i in range(XY):
        part_ref[i] = part

    for copy in stores:
        copy.wait()


def backward_kernel(
    dmixed_hbm, q_hbm, k_hbm, v_hbm, attend_hbm, slope_hbm, dq_hbm, dk_hbm, dv_hbm,
    dmixed, q, k, v, attend, slope, dq, dk, dv, came, went,
):
    pairs = []
    for half in range(2):
        lanes = slice(half * WIDTH // 2, (half + 1) * WIDTH // 2)
        heads = slice(half * HEADS // 2, (half + 1) * HEADS // 2)
        pairs += [(src.at[:, lanes], dst.at[:, lanes]) for src, dst in ((dmixed_hbm, dmixed), (v_hbm, v))]
        pairs += [(src.at[heads], dst.at[heads]) for src, dst in ((slope_hbm, slope), (attend_hbm, attend))]
        pairs += [(src.at[:, lanes], dst.at[:, lanes]) for src, dst in ((k_hbm, k), (q_hbm, q))]
    loads = [pltpu.make_async_copy(src, dst, came.at[i]) for i, (src, dst) in enumerate(pairs)]
    for load in loads:
        load.start()
    stores = []
    for h in range(HEADS):
        if h % 4 == 0:
            for load in loads[h // 4 * 6 : h // 4 * 6 + 6]:
                load.wait()
        lanes = slice(h * HEAD_DIM, (h + 1) * HEAD_DIM)
        part = dmixed[:, lanes]
        dattend = dot(part, v[:, lanes], CONTRACT_LAST)
        dscores = (dattend * slope[h]).astype(BF16)
        dv[:, lanes] = dot(attend[h], part, CONTRACT_FIRST).astype(BF16)
        dq[:, lanes] = dot(dscores, k[:, lanes]).astype(BF16)
        dk[:, lanes] = dot(dscores, q[:, lanes], CONTRACT_FIRST).astype(BF16)
        if h % 2 == 1:
            wide = slice((h - 1) * HEAD_DIM, (h + 1) * HEAD_DIM)
            for src, dst in ((dv, dv_hbm), (dq, dq_hbm), (dk, dk_hbm)):
                copy = pltpu.make_async_copy(src.at[:, wide], dst.at[:, wide], went.at[len(stores)])
                copy.start()
                stores.append(copy)
    for copy in stores:
        copy.wait()


VMEM = pl.BlockSpec(memory_space=pltpu.VMEM)
SMEM = pl.BlockSpec(memory_space=pltpu.SMEM)
ANY = pl.BlockSpec(memory_space=pl.ANY)


def call(kernel, specs, outs, scratch, copies, cost, limit=LIMIT):
    return pl.pallas_call(
        kernel,
        out_shape=[jax.ShapeDtypeStruct(shape, kind) for shape, kind, _ in outs],
        in_specs=specs,
        out_specs=[spec for _, _, spec in outs],
        scratch_shapes=[pltpu.VMEM(shape, kind) for shape, kind in scratch]
        + [pltpu.SemaphoreType.DMA((count,)) for count in copies],
        compiler_params=pltpu.CompilerParams(vmem_limit_bytes=limit),
        cost_estimate=pl.CostEstimate(flops=cost, bytes_accessed=8 * 10**6, transcendentals=524288),
    )


def shift(value, by):
    pairs = []
    for line in range(2 * XY):
        ahead = by if line % 2 == 0 else -by
        pairs += [(line * RING + i, line * RING + (i + ahead) % RING) for i in range(RING)]
    return lax.ppermute(value, ("dp", "pool"), pairs)


TOKEN = (COUNT, WIDTH)
CHUNK = (ROWS, WIDTH)
PAIR = (2 * ROWS, WIDTH)
SQUARES = (HEADS, COUNT, COUNT)
LANES = (COUNT, HEAD_DIM)
TABLE = (POOL, WIDTH)


def body(query_act, key_act, value_act, gate_act, lengths, targets, pool_rows, pool_ids, norm_gain):
    lane = lax.broadcasted_iota(I32, (ROWS, EXTRA), 1)
    column = pool_ids[:, None]
    digits = jnp.where(lane == 0, column // BASE, jnp.where(lane == 1, column % BASE, 0))
    mine = jnp.concatenate([pool_rows, digits.astype(BF16)], axis=1)
    r2 = shift(mine, 2)
    l2 = shift(mine, -2)
    r1 = shift(mine, 1)
    l1 = shift(mine, -1)
    l4 = shift(l2, -2)
    r3 = shift(r2, 1)
    l3 = shift(l2, -1)
    place = lax.axis_index("pool").reshape(1).astype(I32)
    line = lax.axis_index("dp").reshape(1).astype(I32)
    gain = norm_gain.reshape(1, WIDTH)

    emb, normed, aux, attend, slope = call(
        forward_kernel,
        [SMEM] + [ANY] * 4 + [VMEM] * 2,
        [(TOKEN, BF16, ANY), (TOKEN, F32, ANY), (LANES, F32, ANY), (SQUARES, BF16, ANY), (SQUARES, F32, ANY)],
        [(TOKEN, BF16)] * 5 + [(TOKEN, F32), (LANES, F32), (SQUARES, BF16), (SQUARES, F32), ((COUNT, COUNT), F32)],
        (7, HEADS + 5),
        10**9,
    )(lengths, query_act, key_act, value_act, gate_act, gain, targets.reshape(1, COUNT))

    gate_grad, dmixed, part, plus1, minus1, plus4, plus2, minus2, kept = call(
        step_kernel,
        [SMEM, SMEM] + [ANY] * 4 + [VMEM] + [ANY] * 8,
        [(TOKEN, BF16, ANY)] * 2
        + [((XY, 1, WIDTH), F32, VMEM), (PAIR, BF16, ANY), (PAIR, BF16, ANY)]
        + [(CHUNK, BF16, ANY)] * 4,
        [(TOKEN, BF16), ((POOL, WIDTH + EXTRA), BF16), (LANES, F32), (TOKEN, F32), (TOKEN, BF16)]
        + [((COUNT, POOL), F32), ((COUNT, POOL), BF16), (TABLE, BF16), (TOKEN, F32)]
        + [(TOKEN, BF16)] * 2,
        (12, 10),
        2 * 10**9,
    )(place, line, emb, normed, aux, gate_act, gain, mine, r1, r2, r3, l1, l2, l3, l4)

    from_left = shift(plus1, 1)
    from_right = shift(minus1, -1)
    from_far = shift(plus4, 2)
    from_left, from_right, from_far = lax.optimization_barrier((from_left, from_right, from_far))
    plus2 = (plus2.astype(F32) + from_left[:ROWS].astype(F32) + from_far.astype(F32)).astype(BF16)
    minus2 = (minus2.astype(F32) + from_right[:ROWS].astype(F32)).astype(BF16)
    two_left = shift(plus2, 2)
    two_right = shift(minus2, -2)

    plane = [[x * 16 + y * 2 + c for x in range(4) for y in range(8)] for c in range(2)]
    spread = lax.all_to_all(part, "dp", 0, 0, axis_index_groups=plane, tiled=True)
    spread = jnp.broadcast_to(jnp.sum(spread, axis=0, keepdims=True), (NEAR, 1, WIDTH))
    spread, dmixed = lax.optimization_barrier((spread, dmixed))
    near = [[i * NEAR + j for j in range(NEAR)] for i in range(XY)]
    spread = lax.all_to_all(spread, ("dp", "pool"), 0, 0, axis_index_groups=near, tiled=True)
    pool_grad = (
        kept.astype(F32) + from_left[ROWS:].astype(F32) + from_right[ROWS:].astype(F32)
        + two_left.astype(F32) + two_right.astype(F32)
    )
    spread, pool_grad = lax.optimization_barrier((spread, pool_grad))
    gain_grad = jnp.sum(spread, axis=0).reshape(WIDTH)
    dq, dk, dv = call(
        backward_kernel,
        [ANY] * 6,
        [(TOKEN, BF16, ANY)] * 3,
        [(TOKEN, BF16)] * 4 + [(SQUARES, BF16), (SQUARES, F32)] + [(TOKEN, BF16)] * 3,
        (12, 12),
        2 * 10**9,
    )(dmixed, query_act, key_act, value_act, attend, slope)
    return (dq, dk, dv, gate_grad, pool_grad, gain_grad)


def solution(mesh):
    rows = P(("dp", "pool"), None)
    flat = P(("dp", "pool"))
    in_specs = (rows, rows, rows, rows, rows, flat, rows, flat, P())
    out_specs = (rows, rows, rows, rows, rows, P())
    return jax.shard_map(body, mesh=mesh, in_specs=in_specs, out_specs=out_specs, check_vma=False)
```

```python
import jax
import jax.numpy as jnp
from jax import lax
from jax.experimental import pallas as pl
from jax.experimental.pallas import tpu as pltpu
from jax.sharding import PartitionSpec as P

HEADS = 8
LMAX = 192
EPSILON = 1e-05
COUNT = 256
WIDTH = 1024
HEAD_DIM = 128
ROWS = 96
RING = 8
POOL = ROWS * RING
LIMIT = 56 * 1024 * 1024
EXTRA = 128
BASE = 64
XY = 32
NEAR = 16

F32 = jnp.float32
BF16 = jnp.bfloat16
I32 = jnp.int32
CONTRACT_LAST = (((1,), (1,)), ((), ()))
CONTRACT_FIRST = (((0,), (0,)), ((), ()))


def dot(a, b, dims=(((1,), (0,)), ((), ()))):
    return lax.dot_general(a, b, dims, preferred_element_type=F32)


def prepare_kernel(ids_ref, rows_hbm, out_hbm, digits, went):
    rows = pltpu.make_async_copy(rows_hbm, out_hbm.at[:, 0:WIDTH], went.at[0])
    rows.start()
    row = lax.broadcasted_iota(I32, (ROWS, ROWS), 0)
    col = lax.broadcasted_iota(I32, (ROWS, ROWS), 1)
    column = jnp.sum(jnp.where(row == col, ids_ref[...].astype(F32), F32(0.0)), axis=1, keepdims=True)
    upper = jnp.floor(column * F32(1.0 / BASE))
    lane = lax.broadcasted_iota(I32, (ROWS, EXTRA), 1)
    both = jnp.where(lane == 0, upper, jnp.where(lane == 1, column - BASE * upper, F32(0.0)))
    digits[...] = both.astype(BF16)
    tail = pltpu.make_async_copy(digits, out_hbm.at[:, WIDTH : WIDTH + EXTRA], went.at[1])
    tail.start()
    rows.wait()
    tail.wait()


def forward_kernel(
    lengths, q_hbm, k_hbm, v_hbm, gate_hbm, gain_ref, target_ref,
    emb_hbm, normed_hbm, aux_hbm, attend_hbm, slope_hbm,
    q, k, v, gate, emb, normed, aux, attend, slope, mask, came, went,
):
    halves = (slice(0, WIDTH // 2), slice(WIDTH // 2, WIDTH))
    pairs = [
        (src.at[:, half], dst.at[:, half])
        for half in halves
        for src, dst in ((q_hbm, q), (k_hbm, k), (v_hbm, v))
    ] + [(gate_hbm, gate)]
    loads = [pltpu.make_async_copy(src, dst, came.at[i]) for i, (src, dst) in enumerate(pairs)]
    for load in loads:
        load.start()
    stores = []

    def store(src, dst):
        copy = pltpu.make_async_copy(src, dst, went.at[len(stores)])
        copy.start()
        stores.append(copy)

    scaling = HEAD_DIM ** (-0.5)
    row = lax.broadcasted_iota(I32, (COUNT, COUNT), 0)
    col = lax.broadcasted_iota(I32, (COUNT, COUNT), 1)
    first = jnp.zeros((COUNT, COUNT), I32)
    finish = jnp.int32(0)
    for i in range(lengths.shape[1]):
        finish = finish + lengths[0, i]
        first = jnp.where(row >= finish, finish, first)
    mask[...] = jnp.where((col >= first) & (col <= row), F32(1.0 / LMAX), F32(0.0))
    for h in range(HEADS):
        if h % 4 == 0:
            for load in loads[h // 4 * 3 : h // 4 * 3 + 3]:
                load.wait()
        lanes = slice(h * HEAD_DIM, (h + 1) * HEAD_DIM)
        scores = dot(q[:, lanes], k[:, lanes], CONTRACT_LAST) * scaling
        squash = 0.5 * jnp.tanh(0.5 * scores) + 0.5
        keep = mask[...]
        act = scores * squash
        weights = (act * keep).astype(BF16)
        attend[h] = weights
        slope[h] = (squash + act * (1.0 - squash)) * (keep * scaling)
        if h % 2 == 1:
            store(attend.at[h - 1 : h + 1], attend_hbm.at[h - 1 : h + 1])
            store(slope.at[h - 1 : h + 1], slope_hbm.at[h - 1 : h + 1])
        normed[:, lanes] = dot(weights, v[:, lanes])
    loads[6].wait()
    gain = gain_ref[...]
    step = 32
    for i in range(COUNT // step):
        at = slice(i * step, (i + 1) * step)
        part = normed[at, :]
        center = part - jnp.mean(part, axis=1, keepdims=True)
        scale = lax.rsqrt(jnp.mean(center * center, axis=1, keepdims=True) + EPSILON)
        unit = center * scale
        normed[at, :] = unit
        emb[at, :] = (unit * gain * gate[at, :].astype(F32)).astype(BF16)
        lane = lax.broadcasted_iota(I32, (step, HEAD_DIM), 1)
        token = lax.broadcasted_iota(I32, (step, HEAD_DIM), 0) + i * step
        usable = jnp.ones((step, HEAD_DIM), F32)
        finish = jnp.int32(0)
        for j in range(lengths.shape[1]):
            finish = finish + lengths[0, j]
            usable = jnp.where(token + 1 == finish, F32(0.0), usable)
        same = lax.broadcasted_iota(I32, (step, COUNT), 0) + i * step == lax.broadcasted_iota(I32, (step, COUNT), 1)
        target = jnp.sum(jnp.where(same, target_ref[...].astype(F32), F32(0.0)), axis=1, keepdims=True)
        aux[at, :] = jnp.where(lane == 0, scale, jnp.where(lane == 1, usable, target))
        if i % 4 == 3:
            half = slice((i - 3) * step, (i + 1) * step)
            store(normed.at[half], normed_hbm.at[half])
            store(emb.at[half], emb_hbm.at[half])
    store(aux, aux_hbm)
    for copy in stores:
        copy.wait()


def step_kernel(
    place, line, emb_hbm, normed_hbm, aux_hbm, gate_hbm, gain_ref,
    own, r1, r2, r3, l1, l2, l3, l4,
    gate_grad_hbm, dmixed_hbm, part_ref,
    plus1, minus1, plus4, plus2, minus2, kept,
    emb, rows, aux, normed, gate, logits, slopes, terms, back, dmixed, gate_grad, came, went,
):
    z = place[0]
    ahead = 1 - 2 * lax.rem(line[0], 2)

    def start_of(offset):
        return pl.multiple_of(lax.rem(z + ahead * offset + RING, RING) * ROWS, 16)

    stores = []

    def store(src, dst):
        copy = pltpu.make_async_copy(src, dst, went.at[len(stores)])
        copy.start()
        stores.append(copy)

    pairs = [(emb_hbm, emb)]
    for offset, ref in ((0, own), (-1, r1), (-2, r2), (-3, r3), (1, l1), (2, l2), (3, l3), (4, l4)):
        pairs.append((ref, rows.at[pl.ds(start_of(offset), ROWS), :]))
    pairs += [(aux_hbm, aux), (normed_hbm, normed), (gate_hbm, gate)]
    loads = [pltpu.make_async_copy(src, dst, came.at[i]) for i, (src, dst) in enumerate(pairs)]
    for load in loads:
        load.start()
    for load in loads[:10]:
        load.wait()

    logits[...] = dot(emb[...], rows[:, 0:WIDTH], CONTRACT_LAST)
    lane = lax.broadcasted_iota(I32, (8, EXTRA), 1)
    digits = jnp.where(lane == 0, F32(BASE), jnp.where(lane == 1, F32(1.0), F32(0.0))).astype(BF16)
    ids = dot(digits, rows[:, WIDTH : WIDTH + EXTRA], CONTRACT_LAST)[0:1, :]
    step = 32
    for i in range(COUNT // step):
        at = slice(i * step, (i + 1) * step)
        column = lax.broadcasted_iota(I32, (step, POOL), 1).astype(F32)
        chosen = column == aux[at, 2:3]
        own_id = jnp.sum(jnp.where(chosen, ids, F32(0.0)), axis=1, keepdims=True)
        clash = (ids == own_id) & jnp.logical_not(chosen)
        masked = jnp.where(clash, F32(-1e30), logits[at, :])
        peak = jnp.max(masked, axis=1, keepdims=True)
        weight = jnp.where(clash, F32(0.0), jnp.exp(masked - peak))
        total = jnp.sum(weight, axis=1, keepdims=True)
        probs = weight * (1.0 / total)
        slopes[at, :] = (aux[at, 1:2] * jnp.where(chosen, probs - 1.0, probs)).astype(BF16)

    terms[...] = dot(slopes[...], emb[...], CONTRACT_FIRST).astype(BF16)
    for offset, ref in (
        (3, plus1.at[0:ROWS]), (1, plus1.at[ROWS : 2 * ROWS]),
        (-3, minus1.at[0:ROWS]), (-1, minus1.at[ROWS : 2 * ROWS]),
        (4, plus4), (2, plus2), (-2, minus2), (0, kept),
    ):
        store(terms.at[pl.ds(start_of(offset), ROWS), :], ref)

    back[...] = dot(slopes[...], rows[:, 0:WIDTH])
    for load in loads[10:12]:
        load.wait()
    gain = gain_ref[...]
    sums = jnp.zeros((8, WIDTH), F32)
    for i in range(COUNT // step):
        at = slice(i * step, (i + 1) * step)
        unit = normed[at, :]
        pulled = back[at, :]
        gate_grad[at, :] = (pulled * (unit * gain)).astype(BF16)
        dscaled = pulled * gate[at, :].astype(F32)
        product = dscaled * unit
        sums = sums + jnp.sum(product.reshape(step // 8, 8, WIDTH), axis=0)
        dnormed = dscaled * gain
        mean1 = jnp.mean(dnormed, axis=1, keepdims=True)
        mean2 = jnp.mean(product * gain, axis=1, keepdims=True)
        dmixed[at, :] = ((dnormed - mean1 - unit * mean2) * aux[at, 0:1]).astype(BF16)
        if i % 4 == 3:
            half = slice((i - 3) * step, (i + 1) * step)
            store(dmixed.at[half], dmixed_hbm.at[half])
            store(gate_grad.at[half], gate_grad_hbm.at[half])
    part = jnp.sum(sums, axis=0, keepdims=True)
    for i in range(XY):
        part_ref[i] = part

    for copy in stores:
        copy.wait()


def backward_kernel(
    dmixed_hbm, q_hbm, k_hbm, v_hbm, attend_hbm, slope_hbm, dq_hbm, dk_hbm, dv_hbm,
    dmixed, q, k, v, attend, slope, dq, dk, dv, came, went,
):
    pairs = []
    for half in range(2):
        lanes = slice(half * WIDTH // 2, (half + 1) * WIDTH // 2)
        heads = slice(half * HEADS // 2, (half + 1) * HEADS // 2)
        pairs += [(src.at[:, lanes], dst.at[:, lanes]) for src, dst in ((dmixed_hbm, dmixed), (v_hbm, v))]
        pairs += [(src.at[heads], dst.at[heads]) for src, dst in ((slope_hbm, slope), (attend_hbm, attend))]
        pairs += [(src.at[:, lanes], dst.at[:, lanes]) for src, dst in ((k_hbm, k), (q_hbm, q))]
    loads = [pltpu.make_async_copy(src, dst, came.at[i]) for i, (src, dst) in enumerate(pairs)]
    for load in loads:
        load.start()
    stores = []
    for h in range(HEADS):
        if h % 4 == 0:
            for load in loads[h // 4 * 6 : h // 4 * 6 + 6]:
                load.wait()
        lanes = slice(h * HEAD_DIM, (h + 1) * HEAD_DIM)
        part = dmixed[:, lanes]
        dattend = dot(part, v[:, lanes], CONTRACT_LAST)
        dscores = (dattend * slope[h]).astype(BF16)
        dv[:, lanes] = dot(attend[h], part, CONTRACT_FIRST).astype(BF16)
        dq[:, lanes] = dot(dscores, k[:, lanes]).astype(BF16)
        dk[:, lanes] = dot(dscores, q[:, lanes], CONTRACT_FIRST).astype(BF16)
        if h % 2 == 1:
            wide = slice((h - 1) * HEAD_DIM, (h + 1) * HEAD_DIM)
            for src, dst in ((dv, dv_hbm), (dq, dq_hbm), (dk, dk_hbm)):
                copy = pltpu.make_async_copy(src.at[:, wide], dst.at[:, wide], went.at[len(stores)])
                copy.start()
                stores.append(copy)
    for copy in stores:
        copy.wait()


VMEM = pl.BlockSpec(memory_space=pltpu.VMEM)
SMEM = pl.BlockSpec(memory_space=pltpu.SMEM)
ANY = pl.BlockSpec(memory_space=pl.ANY)


def call(kernel, specs, outs, scratch, copies, cost, limit=LIMIT):
    return pl.pallas_call(
        kernel,
        out_shape=[jax.ShapeDtypeStruct(shape, kind) for shape, kind, _ in outs],
        in_specs=specs,
        out_specs=[spec for _, _, spec in outs],
        scratch_shapes=[pltpu.VMEM(shape, kind) for shape, kind in scratch]
        + [pltpu.SemaphoreType.DMA((count,)) for count in copies],
        compiler_params=pltpu.CompilerParams(vmem_limit_bytes=limit),
        cost_estimate=pl.CostEstimate(flops=cost, bytes_accessed=8 * 10**6, transcendentals=524288),
    )


def shift(value, by):
    pairs = []
    for line in range(2 * XY):
        ahead = by if line % 2 == 0 else -by
        pairs += [(line * RING + i, line * RING + (i + ahead) % RING) for i in range(RING)]
    return lax.ppermute(value, ("dp", "pool"), pairs)


TOKEN = (COUNT, WIDTH)
CHUNK = (ROWS, WIDTH)
PAIR = (2 * ROWS, WIDTH)
SQUARES = (HEADS, COUNT, COUNT)
LANES = (COUNT, HEAD_DIM)
TABLE = (POOL, WIDTH)


def body(query_act, key_act, value_act, gate_act, lengths, targets, pool_rows, pool_ids, norm_gain):
    (mine,) = call(
        prepare_kernel,
        [VMEM, ANY],
        [((ROWS, WIDTH + EXTRA), BF16, ANY)],
        [((ROWS, EXTRA), BF16)],
        (2,),
        10**6,
    )(pool_ids.reshape(1, ROWS), pool_rows)
    r2 = shift(mine, 2)
    l2 = shift(mine, -2)
    r1 = shift(mine, 1)
    l1 = shift(mine, -1)
    l4 = shift(l2, -2)
    r3 = shift(r2, 1)
    l3 = shift(l2, -1)
    place = lax.axis_index("pool").reshape(1).astype(I32)
    line = lax.axis_index("dp").reshape(1).astype(I32)
    gain = norm_gain.reshape(1, WIDTH)

    emb, normed, aux, attend, slope = call(
        forward_kernel,
        [SMEM] + [ANY] * 4 + [VMEM] * 2,
        [(TOKEN, BF16, ANY), (TOKEN, F32, ANY), (LANES, F32, ANY), (SQUARES, BF16, ANY), (SQUARES, F32, ANY)],
        [(TOKEN, BF16)] * 5 + [(TOKEN, F32), (LANES, F32), (SQUARES, BF16), (SQUARES, F32), ((COUNT, COUNT), F32)],
        (7, HEADS + 5),
        10**9,
    )(lengths, query_act, key_act, value_act, gate_act, gain, targets.reshape(1, COUNT))

    gate_grad, dmixed, part, plus1, minus1, plus4, plus2, minus2, kept = call(
        step_kernel,
        [SMEM, SMEM] + [ANY] * 4 + [VMEM] + [ANY] * 8,
        [(TOKEN, BF16, ANY)] * 2
        + [((XY, 1, WIDTH), F32, VMEM), (PAIR, BF16, ANY), (PAIR, BF16, ANY)]
        + [(CHUNK, BF16, ANY)] * 4,
        [(TOKEN, BF16), ((POOL, WIDTH + EXTRA), BF16), (LANES, F32), (TOKEN, F32), (TOKEN, BF16)]
        + [((COUNT, POOL), F32), ((COUNT, POOL), BF16), (TABLE, BF16), (TOKEN, F32)]
        + [(TOKEN, BF16)] * 2,
        (12, 12),
        2 * 10**9,
    )(place, line, emb, normed, aux, gate_act, gain, mine, r1, r2, r3, l1, l2, l3, l4)

    from_left = shift(plus1, 1)
    from_right = shift(minus1, -1)
    from_far = shift(plus4, 2)
    from_left, from_right, from_far = lax.optimization_barrier((from_left, from_right, from_far))
    plus2 = (plus2.astype(F32) + from_left[:ROWS].astype(F32) + from_far.astype(F32)).astype(BF16)
    minus2 = (minus2.astype(F32) + from_right[:ROWS].astype(F32)).astype(BF16)
    two_left = shift(plus2, 2)
    two_right = shift(minus2, -2)

    plane = [[x * 16 + y * 2 + c for x in range(4) for y in range(8)] for c in range(2)]
    spread = lax.all_to_all(part, "dp", 0, 0, axis_index_groups=plane, tiled=True)
    spread = jnp.broadcast_to(jnp.sum(spread, axis=0, keepdims=True), (NEAR, 1, WIDTH))
    spread, dmixed = lax.optimization_barrier((spread, dmixed))
    near = [[i * NEAR + j for j in range(NEAR)] for i in range(XY)]
    spread = lax.all_to_all(spread, ("dp", "pool"), 0, 0, axis_index_groups=near, tiled=True)
    pool_grad = (
        kept.astype(F32) + from_left[ROWS:].astype(F32) + from_right[ROWS:].astype(F32)
        + two_left.astype(F32) + two_right.astype(F32)
    )
    spread, pool_grad = lax.optimization_barrier((spread, pool_grad))
    gain_grad = jnp.sum(spread, axis=0).reshape(WIDTH)
    dq, dk, dv = call(
        backward_kernel,
        [ANY] * 6,
        [(TOKEN, BF16, ANY)] * 3,
        [(TOKEN, BF16)] * 4 + [(SQUARES, BF16), (SQUARES, F32)] + [(TOKEN, BF16)] * 3,
        (12, 12),
        2 * 10**9,
    )(dmixed, query_act, key_act, value_act, attend, slope)
    return (dq, dk, dv, gate_grad, pool_grad, gain_grad)


def solution(mesh):
    rows = P(("dp", "pool"), None)
    flat = P(("dp", "pool"))
    in_specs = (rows, rows, rows, rows, rows, flat, rows, flat, P())
    out_specs = (rows, rows, rows, rows, rows, P())
    return jax.shard_map(body, mesh=mesh, in_specs=in_specs, out_specs=out_specs, check_vma=False)
```

```python
import jax
import jax.numpy as jnp
from jax import lax
from jax.experimental import pallas as pl
from jax.experimental.pallas import tpu as pltpu
from jax.sharding import PartitionSpec as P

HEADS = 8
LMAX = 192
EPSILON = 1e-05
COUNT = 256
WIDTH = 1024
HEAD_DIM = 128
ROWS = 96
RING = 8
POOL = ROWS * RING
LIMIT = 56 * 1024 * 1024
EXTRA = 128
BASE = 64
XY = 32
NEAR = 16

F32 = jnp.float32
BF16 = jnp.bfloat16
I32 = jnp.int32
CONTRACT_LAST = (((1,), (1,)), ((), ()))
CONTRACT_FIRST = (((0,), (0,)), ((), ()))


def dot(a, b, dims=(((1,), (0,)), ((), ()))):
    return lax.dot_general(a, b, dims, preferred_element_type=F32)


def prepare_kernel(ids_ref, rows_hbm, out_hbm, wide, went):
    load = pltpu.make_async_copy(rows_hbm, wide.at[:, 0:WIDTH], went.at[0])
    load.start()
    row = lax.broadcasted_iota(I32, (ROWS, ROWS), 0)
    col = lax.broadcasted_iota(I32, (ROWS, ROWS), 1)
    column = jnp.sum(jnp.where(row == col, ids_ref[...].astype(F32), F32(0.0)), axis=1, keepdims=True)
    upper = jnp.floor(column * F32(1.0 / BASE))
    lane = lax.broadcasted_iota(I32, (ROWS, EXTRA), 1)
    both = jnp.where(lane == 0, upper, jnp.where(lane == 1, column - BASE * upper, F32(0.0)))
    wide[:, WIDTH : WIDTH + EXTRA] = both.astype(BF16)
    load.wait()
    store = pltpu.make_async_copy(wide, out_hbm, went.at[1])
    store.start()
    store.wait()


def forward_kernel(
    lengths, q_hbm, k_hbm, v_hbm, gate_hbm, gain_ref, target_ref,
    emb_hbm, normed_hbm, aux_hbm, attend_hbm, slope_hbm,
    q, k, v, gate, emb, normed, aux, attend, slope, mask, came, went,
):
    halves = (slice(0, WIDTH // 2), slice(WIDTH // 2, WIDTH))
    pairs = [
        (src.at[:, half], dst.at[:, half])
        for half in halves
        for src, dst in ((q_hbm, q), (k_hbm, k), (v_hbm, v))
    ] + [(gate_hbm, gate)]
    loads = [pltpu.make_async_copy(src, dst, came.at[i]) for i, (src, dst) in enumerate(pairs)]
    for load in loads:
        load.start()
    stores = []

    def store(src, dst):
        copy = pltpu.make_async_copy(src, dst, went.at[len(stores)])
        copy.start()
        stores.append(copy)

    scaling = HEAD_DIM ** (-0.5)
    row = lax.broadcasted_iota(I32, (COUNT, COUNT), 0)
    col = lax.broadcasted_iota(I32, (COUNT, COUNT), 1)
    first = jnp.zeros((COUNT, COUNT), I32)
    finish = jnp.int32(0)
    for i in range(lengths.shape[1]):
        finish = finish + lengths[0, i]
        first = jnp.where(row >= finish, finish, first)
    mask[...] = jnp.where((col >= first) & (col <= row), F32(1.0 / LMAX), F32(0.0))
    for h in range(HEADS):
        if h % 4 == 0:
            for load in loads[h // 4 * 3 : h // 4 * 3 + 3]:
                load.wait()
        lanes = slice(h * HEAD_DIM, (h + 1) * HEAD_DIM)
        scores = dot(q[:, lanes], k[:, lanes], CONTRACT_LAST) * scaling
        squash = 0.5 * jnp.tanh(0.5 * scores) + 0.5
        keep = mask[...]
        act = scores * squash
        weights = (act * keep).astype(BF16)
        attend[h] = weights
        slope[h] = (squash + act * (1.0 - squash)) * (keep * scaling)
        if h % 2 == 1:
            store(attend.at[h - 1 : h + 1], attend_hbm.at[h - 1 : h + 1])
            store(slope.at[h - 1 : h + 1], slope_hbm.at[h - 1 : h + 1])
        normed[:, lanes] = dot(weights, v[:, lanes])
    loads[6].wait()
    gain = gain_ref[...]
    step = 32
    for i in range(COUNT // step):
        at = slice(i * step, (i + 1) * step)
        part = normed[at, :]
        center = part - jnp.mean(part, axis=1, keepdims=True)
        scale = lax.rsqrt(jnp.mean(center * center, axis=1, keepdims=True) + EPSILON)
        unit = center * scale
        normed[at, :] = unit
        emb[at, :] = (unit * gain * gate[at, :].astype(F32)).astype(BF16)
        lane = lax.broadcasted_iota(I32, (step, HEAD_DIM), 1)
        token = lax.broadcasted_iota(I32, (step, HEAD_DIM), 0) + i * step
        usable = jnp.ones((step, HEAD_DIM), F32)
        finish = jnp.int32(0)
        for j in range(lengths.shape[1]):
            finish = finish + lengths[0, j]
            usable = jnp.where(token + 1 == finish, F32(0.0), usable)
        same = lax.broadcasted_iota(I32, (step, COUNT), 0) + i * step == lax.broadcasted_iota(I32, (step, COUNT), 1)
        target = jnp.sum(jnp.where(same, target_ref[...].astype(F32), F32(0.0)), axis=1, keepdims=True)
        aux[at, :] = jnp.where(lane == 0, scale, jnp.where(lane == 1, usable, target))
        if i % 4 == 3:
            half = slice((i - 3) * step, (i + 1) * step)
            store(normed.at[half], normed_hbm.at[half])
            store(emb.at[half], emb_hbm.at[half])
    store(aux, aux_hbm)
    for copy in stores:
        copy.wait()


def step_kernel(
    place, line, emb_hbm, normed_hbm, aux_hbm, gate_hbm, gain_ref,
    own, r1, r2, r3, l1, l2, l3, l4,
    gate_grad_hbm, dmixed_hbm, part_ref,
    plus1, minus1, plus4, plus2, minus2, kept,
    emb, rows, aux, normed, gate, logits, slopes, terms, back, dmixed, gate_grad, came, went,
):
    z = place[0]
    ahead = 1 - 2 * lax.rem(line[0], 2)

    def start_of(offset):
        return pl.multiple_of(lax.rem(z + ahead * offset + RING, RING) * ROWS, 16)

    stores = []

    def store(src, dst):
        copy = pltpu.make_async_copy(src, dst, went.at[len(stores)])
        copy.start()
        stores.append(copy)

    pairs = [(emb_hbm, emb)]
    for offset, ref in ((0, own), (-1, r1), (-2, r2), (-3, r3), (1, l1), (2, l2), (3, l3), (4, l4)):
        pairs.append((ref, rows.at[pl.ds(start_of(offset), ROWS), :]))
    pairs += [(aux_hbm, aux), (normed_hbm, normed), (gate_hbm, gate)]
    loads = [pltpu.make_async_copy(src, dst, came.at[i]) for i, (src, dst) in enumerate(pairs)]
    for load in loads:
        load.start()
    for load in loads[:10]:
        load.wait()

    logits[...] = dot(emb[...], rows[:, 0:WIDTH], CONTRACT_LAST)
    lane = lax.broadcasted_iota(I32, (8, EXTRA), 1)
    digits = jnp.where(lane == 0, F32(BASE), jnp.where(lane == 1, F32(1.0), F32(0.0))).astype(BF16)
    ids = dot(digits, rows[:, WIDTH : WIDTH + EXTRA], CONTRACT_LAST)[0:1, :]
    step = 32
    for i in range(COUNT // step):
        at = slice(i * step, (i + 1) * step)
        column = lax.broadcasted_iota(I32, (step, POOL), 1).astype(F32)
        chosen = column == aux[at, 2:3]
        own_id = jnp.sum(jnp.where(chosen, ids, F32(0.0)), axis=1, keepdims=True)
        clash = (ids == own_id) & jnp.logical_not(chosen)
        masked = jnp.where(clash, F32(-1e30), logits[at, :])
        peak = jnp.max(masked, axis=1, keepdims=True)
        weight = jnp.where(clash, F32(0.0), jnp.exp(masked - peak))
        total = jnp.sum(weight, axis=1, keepdims=True)
        probs = weight * (1.0 / total)
        slopes[at, :] = (aux[at, 1:2] * jnp.where(chosen, probs - 1.0, probs)).astype(BF16)

    terms[...] = dot(slopes[...], emb[...], CONTRACT_FIRST).astype(BF16)
    for offset, ref in (
        (3, plus1.at[0:ROWS]), (1, plus1.at[ROWS : 2 * ROWS]),
        (-3, minus1.at[0:ROWS]), (-1, minus1.at[ROWS : 2 * ROWS]),
        (4, plus4), (2, plus2), (-2, minus2), (0, kept),
    ):
        store(terms.at[pl.ds(start_of(offset), ROWS), :], ref)

    back[...] = dot(slopes[...], rows[:, 0:WIDTH])
    for load in loads[10:12]:
        load.wait()
    gain = gain_ref[...]
    sums = jnp.zeros((8, WIDTH), F32)
    for i in range(COUNT // step):
        at = slice(i * step, (i + 1) * step)
        unit = normed[at, :]
        pulled = back[at, :]
        gate_grad[at, :] = (pulled * (unit * gain)).astype(BF16)
        dscaled = pulled * gate[at, :].astype(F32)
        product = dscaled * unit
        sums = sums + jnp.sum(product.reshape(step // 8, 8, WIDTH), axis=0)
        dnormed = dscaled * gain
        mean1 = jnp.mean(dnormed, axis=1, keepdims=True)
        mean2 = jnp.mean(product * gain, axis=1, keepdims=True)
        dmixed[at, :] = ((dnormed - mean1 - unit * mean2) * aux[at, 0:1]).astype(BF16)
        if i % 4 == 3:
            half = slice((i - 3) * step, (i + 1) * step)
            store(dmixed.at[half], dmixed_hbm.at[half])
            store(gate_grad.at[half], gate_grad_hbm.at[half])
    part = jnp.sum(sums, axis=0, keepdims=True)
    for i in range(XY):
        part_ref[i] = part

    for copy in stores:
        copy.wait()


def backward_kernel(
    dmixed_hbm, q_hbm, k_hbm, v_hbm, attend_hbm, slope_hbm, dq_hbm, dk_hbm, dv_hbm,
    dmixed, q, k, v, attend, slope, dq, dk, dv, came, went,
):
    pairs = []
    for half in range(2):
        lanes = slice(half * WIDTH // 2, (half + 1) * WIDTH // 2)
        heads = slice(half * HEADS // 2, (half + 1) * HEADS // 2)
        pairs += [(src.at[:, lanes], dst.at[:, lanes]) for src, dst in ((dmixed_hbm, dmixed), (v_hbm, v))]
        pairs += [(src.at[heads], dst.at[heads]) for src, dst in ((slope_hbm, slope), (attend_hbm, attend))]
        pairs += [(src.at[:, lanes], dst.at[:, lanes]) for src, dst in ((k_hbm, k), (q_hbm, q))]
    loads = [pltpu.make_async_copy(src, dst, came.at[i]) for i, (src, dst) in enumerate(pairs)]
    for load in loads:
        load.start()
    stores = []
    for h in range(HEADS):
        if h % 4 == 0:
            for load in loads[h // 4 * 6 : h // 4 * 6 + 6]:
                load.wait()
        lanes = slice(h * HEAD_DIM, (h + 1) * HEAD_DIM)
        part = dmixed[:, lanes]
        dattend = dot(part, v[:, lanes], CONTRACT_LAST)
        dscores = (dattend * slope[h]).astype(BF16)
        dv[:, lanes] = dot(attend[h], part, CONTRACT_FIRST).astype(BF16)
        dq[:, lanes] = dot(dscores, k[:, lanes]).astype(BF16)
        dk[:, lanes] = dot(dscores, q[:, lanes], CONTRACT_FIRST).astype(BF16)
        if h % 2 == 1:
            wide = slice((h - 1) * HEAD_DIM, (h + 1) * HEAD_DIM)
            for src, dst in ((dv, dv_hbm), (dq, dq_hbm), (dk, dk_hbm)):
                copy = pltpu.make_async_copy(src.at[:, wide], dst.at[:, wide], went.at[len(stores)])
                copy.start()
                stores.append(copy)
    for copy in stores:
        copy.wait()


VMEM = pl.BlockSpec(memory_space=pltpu.VMEM)
SMEM = pl.BlockSpec(memory_space=pltpu.SMEM)
ANY = pl.BlockSpec(memory_space=pl.ANY)


def call(kernel, specs, outs, scratch, copies, cost, limit=LIMIT):
    return pl.pallas_call(
        kernel,
        out_shape=[jax.ShapeDtypeStruct(shape, kind) for shape, kind, _ in outs],
        in_specs=specs,
        out_specs=[spec for _, _, spec in outs],
        scratch_shapes=[pltpu.VMEM(shape, kind) for shape, kind in scratch]
        + [pltpu.SemaphoreType.DMA((count,)) for count in copies],
        compiler_params=pltpu.CompilerParams(vmem_limit_bytes=limit),
        cost_estimate=pl.CostEstimate(flops=cost, bytes_accessed=8 * 10**6, transcendentals=524288),
    )


def shift(value, by):
    pairs = []
    for line in range(2 * XY):
        ahead = by if line % 2 == 0 else -by
        pairs += [(line * RING + i, line * RING + (i + ahead) % RING) for i in range(RING)]
    return lax.ppermute(value, ("dp", "pool"), pairs)


TOKEN = (COUNT, WIDTH)
CHUNK = (ROWS, WIDTH)
PAIR = (2 * ROWS, WIDTH)
SQUARES = (HEADS, COUNT, COUNT)
LANES = (COUNT, HEAD_DIM)
TABLE = (POOL, WIDTH)


def body(query_act, key_act, value_act, gate_act, lengths, targets, pool_rows, pool_ids, norm_gain):
    (mine,) = call(
        prepare_kernel,
        [VMEM, ANY],
        [((ROWS, WIDTH + EXTRA), BF16, ANY)],
        [((ROWS, WIDTH + EXTRA), BF16)],
        (2,),
        10**6,
    )(pool_ids.reshape(1, ROWS), pool_rows)
    r2 = shift(mine, 2)
    l2 = shift(mine, -2)
    r1 = shift(mine, 1)
    l1 = shift(mine, -1)
    l4 = shift(l2, -2)
    r3 = shift(r2, 1)
    l3 = shift(l2, -1)
    place = lax.axis_index("pool").reshape(1).astype(I32)
    line = lax.axis_index("dp").reshape(1).astype(I32)
    gain = norm_gain.reshape(1, WIDTH)

    emb, normed, aux, attend, slope = call(
        forward_kernel,
        [SMEM] + [ANY] * 4 + [VMEM] * 2,
        [(TOKEN, BF16, ANY), (TOKEN, F32, ANY), (LANES, F32, ANY), (SQUARES, BF16, ANY), (SQUARES, F32, ANY)],
        [(TOKEN, BF16)] * 5 + [(TOKEN, F32), (LANES, F32), (SQUARES, BF16), (SQUARES, F32), ((COUNT, COUNT), F32)],
        (7, HEADS + 5),
        10**9,
    )(lengths, query_act, key_act, value_act, gate_act, gain, targets.reshape(1, COUNT))

    gate_grad, dmixed, part, plus1, minus1, plus4, plus2, minus2, kept = call(
        step_kernel,
        [SMEM, SMEM] + [ANY] * 4 + [VMEM] + [ANY] * 8,
        [(TOKEN, BF16, ANY)] * 2
        + [((XY, 1, WIDTH), F32, VMEM), (PAIR, BF16, ANY), (PAIR, BF16, ANY)]
        + [(CHUNK, BF16, ANY)] * 4,
        [(TOKEN, BF16), ((POOL, WIDTH + EXTRA), BF16), (LANES, F32), (TOKEN, F32), (TOKEN, BF16)]
        + [((COUNT, POOL), F32), ((COUNT, POOL), BF16), (TABLE, BF16), (TOKEN, F32)]
        + [(TOKEN, BF16)] * 2,
        (12, 12),
        2 * 10**9,
    )(place, line, emb, normed, aux, gate_act, gain, mine, r1, r2, r3, l1, l2, l3, l4)

    from_left = shift(plus1, 1)
    from_right = shift(minus1, -1)
    from_far = shift(plus4, 2)
    from_left, from_right, from_far = lax.optimization_barrier((from_left, from_right, from_far))
    plus2 = (plus2.astype(F32) + from_left[:ROWS].astype(F32) + from_far.astype(F32)).astype(BF16)
    minus2 = (minus2.astype(F32) + from_right[:ROWS].astype(F32)).astype(BF16)
    two_left = shift(plus2, 2)
    two_right = shift(minus2, -2)

    plane = [[x * 16 + y * 2 + c for x in range(4) for y in range(8)] for c in range(2)]
    spread = lax.all_to_all(part, "dp", 0, 0, axis_index_groups=plane, tiled=True)
    spread = jnp.broadcast_to(jnp.sum(spread, axis=0, keepdims=True), (NEAR, 1, WIDTH))
    spread, dmixed = lax.optimization_barrier((spread, dmixed))
    near = [[i * NEAR + j for j in range(NEAR)] for i in range(XY)]
    spread = lax.all_to_all(spread, ("dp", "pool"), 0, 0, axis_index_groups=near, tiled=True)
    pool_grad = (
        kept.astype(F32) + from_left[ROWS:].astype(F32) + from_right[ROWS:].astype(F32)
        + two_left.astype(F32) + two_right.astype(F32)
    )
    spread, pool_grad = lax.optimization_barrier((spread, pool_grad))
    gain_grad = jnp.sum(spread, axis=0).reshape(WIDTH)
    dq, dk, dv = call(
        backward_kernel,
        [ANY] * 6,
        [(TOKEN, BF16, ANY)] * 3,
        [(TOKEN, BF16)] * 4 + [(SQUARES, BF16), (SQUARES, F32)] + [(TOKEN, BF16)] * 3,
        (12, 12),
        2 * 10**9,
    )(dmixed, query_act, key_act, value_act, attend, slope)
    return (dq, dk, dv, gate_grad, pool_grad, gain_grad)


def solution(mesh):
    rows = P(("dp", "pool"), None)
    flat = P(("dp", "pool"))
    in_specs = (rows, rows, rows, rows, rows, flat, rows, flat, P())
    out_specs = (rows, rows, rows, rows, rows, P())
    return jax.shard_map(body, mesh=mesh, in_specs=in_specs, out_specs=out_specs, check_vma=False)
```
